512 devices in a mesh: ctx: 64 (over z, y), grp: 8 (over x, core).
Axes of the slice: x: 4, y: 4, z: 16, core: 2. Of those that a mesh axis runs over, the one named last changes fastest.
Arguments:
- query_nope: bfloat16 [64, 128, 128], P('grp', 'ctx'), parts along dimension 0, may hold values from -6 to 6
- query_rope: bfloat16 [64, 128, 64], P('grp', 'ctx'), parts along dimension 0, may hold values from -20 to 20
- weight_key: bfloat16 [128, 128, 512], P('ctx'), may hold values from -0.5 to 0.5
- weight_value: bfloat16 [128, 512, 128], P('ctx'), may hold values from -0.25 to 0.25
- cache_codes: bfloat16 [64, 24576, 512], P('grp', 'ctx'), parts along dimension 0, may hold values from -6 to 6
- cache_rope: bfloat16 [64, 24576, 64], P('grp', 'ctx'), parts along dimension 0, may hold values from -6 to 6
- cache_scale: float32 [64, 24576], P('grp', 'ctx'), parts along dimension 0, may hold values from 0.25 to 16, as said below
- lengths: int32 [64], P('grp'), parts along dimension 0, may hold values from 8192 to 24576, as said below
- tile_live: int32 [64, 192], P('grp', 'ctx'), parts along dimension 0, may hold values from 0 to 1, as said below
Outputs:
- attended: bfloat16 [64, 128, 128], P('grp', 'ctx'), parts along dimension 0
The draws below stay inside these ranges and needn't reach their ends.
There are 8 independent parts, one for each index of `grp`. The reference program is written for one: setup_inputs(seed, part) draws one part's arguments, and reference() takes and returns one part's arrays. A program takes and returns all parts, laid end to end along the dimension named above; an argument that names none is the same for every part. Nothing has to cross between parts.
Inputs may be any that keep to these rules, and one draw needn't show every extreme that they name: `lengths`: every request's length is at least S // 3. `tile_live`: the first tile of every request is kept; tiles at or beyond a request's length are 0. `cache_scale`: positive scales.
All inputs are finite; a program needn't handle non-finite values.
Results may differ from the reference program's by a relative error of at most 0.012.
The reference program's roundings to bfloat16 on the way (of `query_latent`, `probs` and `latent_out`) count: a program that leaves them out, or rounds other values in their place, can miss the bound.
Values may be sent and summed in bfloat16 or wider, within the bound.
A program may use at most 64 MiB of HBM per device.

```python
import jax
import jax.numpy as jnp
from jax import lax

H = 128
DL = 512
DR = 64
DN = 128
DV = 128
B = 8
TILE = 128
S = 24576
NT = 192


def shared_lengths(key):
    first, second = jax.random.split(key)
    drawn = jax.random.randint(first, (B,), S // 3, S + 1)
    chosen = jax.random.randint(second, (), 0, B)
    drawn = jnp.where(jnp.arange(B) == chosen, S, drawn)
    return drawn.astype(jnp.int32)


def rotary_pattern(key):
    key = jax.random.fold_in(key, 101)
    first, second, third = jax.random.split(key, 3)
    signs = jnp.where(jax.random.bernoulli(first, 0.5, (DR,)), 1.0, -1.0).astype(jnp.float32)
    offset = jax.random.randint(second, (), 0, 8)
    places = jax.random.randint(third, (B,), 1, TILE // 2)
    return (signs, offset, places)


def base_values(key, shape, spread):
    return jnp.clip(jax.random.normal(key, shape, jnp.float32), -spread, spread)


def draw_lengths(key, part):
    return shared_lengths(key)


def draw_tile_live(key, part):
    drawn = shared_lengths(key)
    key = jax.random.fold_in(key, 7)
    keeping = jax.random.randint(key, (B, NT), 0, 8) > 0
    tile_ids = jnp.arange(NT)
    starts = tile_ids * TILE
    live = (starts[None, :] < drawn[:, None]) & (keeping | (tile_ids == 0)[None, :])
    return live.astype(jnp.int32)


def draw_cache_scale(key, part):
    key = jax.random.fold_in(key, 11)
    lower, upper = (0.25, 2.0)
    uniform_draw = jax.random.uniform(key, (B, S), jnp.float32)
    return jnp.exp(jnp.log(lower) + uniform_draw * (jnp.log(upper) - jnp.log(lower)))


def draw_query_rope(key, part):
    signs, offset, places = rotary_pattern(key)
    key = jax.random.fold_in(key, 21)
    base = base_values(key, (B, H, DR), 6.0)
    heads = jnp.arange(H)
    strong = (heads + offset) % 8 == 0
    levels = jnp.array([7.0, 11.0, 16.0, 20.0], jnp.float32)[heads // 8 % 4]
    strength = levels * 64.0 / DR
    planted = strength[None, :, None] * signs[None, None, :]
    return jnp.where(strong[None, :, None], planted, base).astype(jnp.bfloat16)


def draw_cache_rope(key, part):
    signs, offset, places = rotary_pattern(key)
    key = jax.random.fold_in(key, 23)
    base = base_values(key, (B, S, DR), 6.0)
    positions = jnp.arange(S)
    near = (positions[None, :] == places[:, None])[:, :, None]
    second = (positions[None, :] == places[:, None] + TILE // 2)[:, :, None]
    rows = jnp.where(second, 4.0 * (1.0 - 0.0075) * signs[None, None, :], base)
    return jnp.where(near, 4.0 * signs[None, None, :], rows).astype(jnp.bfloat16)


def level_of(rng, extent, cuts, low, high):
    def one(position, blocks):
        steps = jax.random.uniform(jax.random.fold_in(jax.random.fold_in(rng, 6), position), (blocks,), jnp.float32, low / len(cuts), high / len(cuts))
        return jnp.repeat(jnp.exp(steps), extent[position] // blocks).reshape((-1,) + (1,) * (len(extent) - position - 1))

    level = one(*cuts[0])
    for cut in cuts[1:]:
        level = level * one(*cut)
    return level


def centred(key, dims, width, bound, shards=(), kind=jnp.bfloat16):
    gain = level_of(key, dims, shards, -0.22, 0.18) if shards else 1.0
    entries = jax.random.normal(key, dims, jnp.float32) * width * gain
    return jnp.minimum(jnp.maximum(entries, -bound), bound).astype(kind)


def setup_inputs(seed: int = 0, part: int = 0) -> dict:
    arg_keys = jax.random.split(jax.random.key(seed), 10)
    part_keys = jax.random.split(jax.random.fold_in(arg_keys[9], part), 10)
    return {
        "query_nope": centred(part_keys[0], (B, H, DN), 1.0, 6.0, ((1, 64),)),
        "query_rope": draw_query_rope(jax.random.fold_in(jax.random.fold_in(arg_keys[9], part), 71), part),
        "weight_key": centred(arg_keys[2], (H, DN, DL), DN ** -0.5, 0.5, ((0, 64),)),
        "weight_value": centred(arg_keys[3], (H, DL, DV), DL ** -0.5, 0.25, ((0, 64),)),
        "cache_codes": centred(part_keys[4], (B, S, DL), 1.0, 6.0, ((1, 64),)),
        "cache_rope": draw_cache_rope(jax.random.fold_in(jax.random.fold_in(arg_keys[9], part), 71), part),
        "cache_scale": draw_cache_scale(jax.random.fold_in(jax.random.fold_in(arg_keys[9], part), 71), part),
        "lengths": draw_lengths(jax.random.fold_in(jax.random.fold_in(arg_keys[9], part), 71), part),
        "tile_live": draw_tile_live(jax.random.fold_in(jax.random.fold_in(arg_keys[9], part), 71), part),
    }


score_factor = 0.0721688


def reference(query_nope, query_rope, weight_key, weight_value, cache_codes, cache_rope, cache_scale, lengths, tile_live):
    query_latent = jnp.einsum("bhn,hnl->bhl", query_nope.astype(jnp.float32), weight_key.astype(jnp.float32)).astype(jnp.bfloat16)
    positions = jnp.arange(S, dtype=jnp.int32)

    def request(items):
        latent, rotary, codes, keys, scales, length, live = items
        kept = jnp.repeat(live, TILE) == 1
        valid = (positions < length) & kept
        part_latent = jnp.dot(latent, codes.T, preferred_element_type=jnp.float32)
        part_rope = jnp.dot(rotary, keys.T, preferred_element_type=jnp.float32)
        scores = score_factor * (scales[None, :] * part_latent + part_rope)
        masked = jnp.where(valid[None, :], scores, jnp.float32(-1e30))
        top = jnp.max(masked, axis=1, keepdims=True)
        expo = jnp.where(valid[None, :], jnp.exp(masked - top), jnp.float32(0.0))
        total = jnp.sum(expo, axis=1, keepdims=True)
        probs = (expo * scales[None, :]).astype(jnp.bfloat16)
        summed = jnp.dot(probs, codes, preferred_element_type=jnp.float32)
        return (summed / total).astype(jnp.bfloat16)

    latent_out = lax.map(request, (query_latent, query_rope, cache_codes, cache_rope, cache_scale, lengths, tile_live))
    attended = jnp.einsum("bhl,hlv->bhv", latent_out.astype(jnp.float32), weight_value.astype(jnp.float32))
    return attended.astype(jnp.bfloat16)
```

```python
import functools

import jax
import jax.numpy as jnp
from jax import lax
from jax.experimental import pallas as pl
from jax.experimental.pallas import tpu as pltpu
from jax.sharding import PartitionSpec as P

score_factor = 0.0721688
NZ, NY = 16, 4
B, DL, DR, DN, DV = 8, 512, 64, 128, 128
SLOTS, TILE = 384, 128
QW = 640
MESH = pl.DeviceIdType.MESH
Z_OFFS = (8, 7, -7, 6, -6, 5, -5, 4, -4, 3, -3, 2, -2, 1, -1)
Y_OFFS = (2, 1, -1)
f32 = jnp.float32
bf16 = jnp.bfloat16


def kernel(
    q_ref, wk_hbm, wv_hbm, codes_hbm, rope_hbm, scale_ref, len_ref, live_ref, out_ref,
    wk, wv, codes, rope, zbuf, zf, qbuf, obuf, rbuf, sbuf, srbuf, zr, zsend, zrecv, tsend, trecv,
    load_sem, zs, zrs, ys, yr, ps, pr, pss, psr, os_, or_, oss, osr,
):
    me = lax.axis_index("ctx")
    z, y = me // NY, lax.rem(me, NY)

    def zdev(k):
        return {"ctx": lax.rem(z + k + NZ, NZ) * NY + y}

    def ydev(k):
        return {"ctx": z * NY + lax.rem(y + k + NY, NY)}

    def load(i):
        if i == 0:
            return pltpu.make_async_copy(wk_hbm, wk, load_sem.at[0])
        if i == 1:
            return pltpu.make_async_copy(codes_hbm, codes, load_sem.at[1])
        if i == 2:
            return pltpu.make_async_copy(rope_hbm, rope, load_sem.at[2])
        return pltpu.make_async_copy(wv_hbm, wv, load_sem.at[3])

    for i in range(4):
        load(i).start()

    barrier = pltpu.get_barrier_semaphore()
    for k in Z_OFFS:
        pl.semaphore_signal(barrier, inc=1, device_id=zdev(k), device_id_type=MESH)
    for k in Y_OFFS:
        pl.semaphore_signal(barrier, inc=1, device_id=ydev(k), device_id_type=MESH)

    load(0).wait()
    latent = jnp.concatenate(
        [jnp.dot(q_ref[h, :, :DN], wk[h], preferred_element_type=f32) for h in range(2)], axis=0
    )
    zbuf[z, :, :DL] = latent.astype(bf16)
    zbuf[z, :, DL:] = jnp.concatenate([q_ref[h, :, DN:].astype(f32) for h in range(2)], axis=0).astype(bf16)

    pl.semaphore_wait(barrier, len(Z_OFFS) + len(Y_OFFS))

    def zcopy(i):
        return pltpu.make_async_remote_copy(
            zbuf.at[z], zbuf.at[z], zs.at[i], zrs.at[i], device_id=zdev(Z_OFFS[i]), device_id_type=MESH
        )

    for i in range(len(Z_OFFS)):
        zcopy(i).start()
    for i in range(len(Z_OFFS)):
        zcopy(i).wait_recv()
    for s in range(NZ):
        for j in range(QW // 128):
            zf[j, pl.ds(s * 16, 16), :] = zbuf[s, :, j * 128 : (j + 1) * 128].astype(f32)

    def ycopy(b, i):
        return pltpu.make_async_remote_copy(
            qbuf.at[b, y], qbuf.at[b, y], ys.at[b, i], yr.at[b, i],
            device_id=ydev(Y_OFFS[i]), device_id_type=MESH,
        )

    def spread(b, c):
        for j in range(QW // 128):
            qbuf[b, y, :, pl.ds(j * 128, 128)] = zf[j, pl.ds(b, 32, stride=8), :].astype(bf16)
        for i in range(3):
            ycopy(b, i).start()
        return c

    lax.fori_loop(0, B, spread, 0)
    load(1).wait()
    load(2).wait()

    def pcopy(b, i):
        return pltpu.make_async_remote_copy(
            obuf.at[b, lax.rem(y + Y_OFFS[i] + NY, NY)], rbuf.at[b, i], ps.at[b, i], pr.at[b, i],
            device_id=ydev(Y_OFFS[i]), device_id_type=MESH,
        )

    def scopy(b, i):
        return pltpu.make_async_remote_copy(
            sbuf.at[b], srbuf.at[b, i], pss.at[b, i], psr.at[b, i],
            device_id=ydev(Y_OFFS[i]), device_id_type=MESH,
        )

    lane = lax.broadcasted_iota(jnp.int32, (1, TILE), 1)
    heads = NY * 32
    eye = lax.broadcasted_iota(jnp.int32, (heads, heads), 0) == lax.broadcasted_iota(
        jnp.int32, (heads, heads), 1
    )

    def attend(b, c):
        for i in range(3):
            ycopy(b, i).wait_recv()
        q = qbuf[b].reshape(heads, QW)
        nt = (((1,), (1,)), ((), ()))
        codes_b = codes[b]
        part = lax.dot_general(q[:, :DL], codes_b, nt, preferred_element_type=f32)
        turned = lax.dot_general(q[:, DL : DL + DR], rope[b], nt, preferred_element_type=f32)
        scale = scale_ref[pl.ds(b, 1), :]
        length = len_ref[b]
        flags = []
        for t in range(SLOTS // TILE):
            limit = jnp.where(live_ref[b, t] == 1, length - (me * SLOTS + t * TILE), 0)
            flags.append(jnp.where(lane < limit, f32(1.0), f32(0.0)))
        valid = jnp.concatenate(flags, axis=1) > 0.5
        scores = score_factor * (scale * part + turned)
        masked = jnp.where(valid, scores, f32(-1e30))
        top = jnp.max(masked, axis=1, keepdims=True)
        expo = jnp.where(valid, jnp.exp(masked - top), f32(0.0))
        total = jnp.sum(expo, axis=1, keepdims=True)
        probs = (expo * scale).astype(bf16)
        summed = jnp.dot(probs, codes_b, preferred_element_type=f32)
        obuf[b] = summed.astype(bf16).reshape(NY, 32, DL)
        sbuf[b, pl.ds(0, 1), :] = jnp.sum(jnp.where(eye, top, f32(0.0)), axis=0, keepdims=True)
        sbuf[b, pl.ds(1, 1), :] = jnp.sum(jnp.where(eye, total, f32(0.0)), axis=0, keepdims=True)
        for i in range(3):
            pcopy(b, i).start()
            scopy(b, i).start()
        return c

    lax.fori_loop(0, B, attend, 0)

    rows32 = lax.broadcasted_iota(jnp.int32, (32, 128), 0)
    lanes32 = lax.broadcasted_iota(jnp.int32, (32, 128), 1)
    pick = lanes32 == rows32 + y * 32

    def column(row):
        return jnp.sum(jnp.where(pick, row, f32(0.0)), axis=1, keepdims=True)

    def combine(b, stats):
        for i in range(3):
            pcopy(b, i).wait_recv()
            scopy(b, i).wait_recv()
        tops = [column(sbuf[b, pl.ds(0, 1), :])] + [column(srbuf[b, i, pl.ds(0, 1), :]) for i in range(3)]
        totals = [column(sbuf[b, pl.ds(1, 1), :])] + [column(srbuf[b, i, pl.ds(1, 1), :]) for i in range(3)]
        top = functools.reduce(jnp.maximum, tops)
        factors = [jnp.exp(t - top) for t in tops]
        total = sum(f * t for f, t in zip(factors, totals))
        summed = factors[0] * obuf[b, y].astype(f32)
        for i in range(3):
            summed = summed + factors[i + 1] * rbuf[b, i].astype(f32)
        for j in range(DL // 128):
            zr[j, pl.ds(b, 32, stride=8), :] = summed[:, j * 128 : (j + 1) * 128]
        stats = jnp.where(lanes32 == b, top, stats)
        return jnp.where(lanes32 == B + b, total, stats)

    stats = lax.fori_loop(0, B, combine, jnp.zeros((32, 128), f32))
    for s in range(NZ):
        for j in range(DL // 128):
            zsend[s, :, j * 128 : (j + 1) * 128] = zr[j, pl.ds(s * 16, 16), :].astype(bf16)
        tsend[s] = stats[s * 2 : s * 2 + 2, :]

    def ocopy(i):
        k = Z_OFFS[i]
        return pltpu.make_async_remote_copy(
            zsend.at[lax.rem(z + k + NZ, NZ)], zrecv.at[i], os_.at[i], or_.at[i],
            device_id=zdev(k), device_id_type=MESH,
        )

    def tcopy(i):
        k = Z_OFFS[i]
        return pltpu.make_async_remote_copy(
            tsend.at[lax.rem(z + k + NZ, NZ)], trecv.at[i], oss.at[i], osr.at[i],
            device_id=zdev(k), device_id_type=MESH,
        )

    for i in range(len(Z_OFFS)):
        ocopy(i).start()
        tcopy(i).start()

    rows16 = lax.broadcasted_iota(jnp.int32, (8, 128), 0)
    lanes16 = lax.broadcasted_iota(jnp.int32, (8, 128), 1)

    def column16(two, first):
        return jnp.concatenate(
            [
                jnp.sum(jnp.where(lanes16 == rows16 + first, two[h : h + 1, :], f32(0.0)), axis=1, keepdims=True)
                for h in range(2)
            ],
            axis=0,
        )

    load(3).wait()
    for i in range(len(Z_OFFS)):
        tcopy(i).wait_recv()
    pairs = [tsend[z]] + [trecv[i] for i in range(len(Z_OFFS))]
    tops = [column16(p, 0) for p in pairs]
    totals = [column16(p, B) for p in pairs]
    top = functools.reduce(jnp.maximum, tops)
    factors = [jnp.exp(t - top) for t in tops]
    total = sum(f * t for f, t in zip(factors, totals))
    for i in range(len(Z_OFFS)):
        ocopy(i).wait_recv()
    summed = factors[0] * zsend[z].astype(f32)
    for i in range(len(Z_OFFS)):
        summed = summed + factors[i + 1] * zrecv[i].astype(f32)
    latent_out = (summed / total).astype(bf16)
    for h in range(2):
        out_ref[h] = jnp.dot(
            latent_out[h * 8 : h * 8 + 8, :], wv[h], preferred_element_type=f32
        ).astype(bf16)

    for i in range(len(Z_OFFS)):
        zcopy(i).wait_send()
        ocopy(i).wait_send()
        tcopy(i).wait_send()

    def drain(b, c):
        for i in range(3):
            ycopy(b, i).wait_send()
            pcopy(b, i).wait_send()
            scopy(b, i).wait_send()
        return c

    lax.fori_loop(0, B, drain, 0)


def per_device(
    query_nope, query_rope, weight_key, weight_value, cache_codes, cache_rope, cache_scale, lengths, tile_live
):
    pad = jnp.zeros((B, 2, 64), bf16)
    query = jnp.concatenate([query_nope, query_rope, pad], axis=2).transpose(1, 0, 2)
    hbm = pl.BlockSpec(memory_space=pl.ANY)
    vmem = pl.BlockSpec(memory_space=pltpu.VMEM)
    smem = pl.BlockSpec(memory_space=pltpu.SMEM)
    dma = pltpu.SemaphoreType.DMA
    n = len(Z_OFFS)
    out = pl.pallas_call(
        kernel,
        out_shape=jax.ShapeDtypeStruct((2, B, DV), bf16),
        in_specs=[vmem, hbm, hbm, hbm, hbm, vmem, smem, smem],
        out_specs=vmem,
        scratch_shapes=[
            pltpu.VMEM((2, DN, DL), bf16),
            pltpu.VMEM((2, DL, DV), bf16),
            pltpu.VMEM((B, SLOTS, DL), bf16),
            pltpu.VMEM((B, SLOTS, DR), bf16),
            pltpu.VMEM((NZ, 16, QW), bf16),
            pltpu.VMEM((QW // 128, NZ * 16, 128), f32),
            pltpu.VMEM((B, NY, 32, QW), bf16),
            pltpu.VMEM((B, NY, 32, DL), bf16),
            pltpu.VMEM((B, 3, 32, DL), bf16),
            pltpu.VMEM((B, 2, 128), f32),
            pltpu.VMEM((B, 3, 2, 128), f32),
            pltpu.VMEM((DL // 128, NZ * 16, 128), f32),
            pltpu.VMEM((NZ, 16, DL), bf16),
            pltpu.VMEM((n, 16, DL), bf16),
            pltpu.VMEM((NZ, 2, 128), f32),
            pltpu.VMEM((n, 2, 128), f32),
            dma((4,)),
            dma((n,)), dma((n,)),
            dma((B, 3)), dma((B, 3)),
            dma((B, 3)), dma((B, 3)),
            dma((B, 3)), dma((B, 3)),
            dma((n,)), dma((n,)),
            dma((n,)), dma((n,)),
        ],
        compiler_params=pltpu.CompilerParams(
            collective_id=0, has_side_effects=True, vmem_limit_bytes=40 * 1024 * 1024
        ),
        cost_estimate=pl.CostEstimate(flops=860_000_000, bytes_accessed=4_500_000, transcendentals=400_000),
        name="latent_decode",
    )(query, weight_key, weight_value, cache_codes, cache_rope, cache_scale, lengths, tile_live)
    return out.transpose(1, 0, 2)


def solution(mesh):
    in_specs = (
        P("grp", "ctx", None),
        P("grp", "ctx", None),
        P("ctx", None, None),
        P("ctx", None, None),
        P("grp", "ctx", None),
        P("grp", "ctx", None),
        P("grp", "ctx"),
        P("grp"),
        P("grp", "ctx"),
    )
    return jax.shard_map(
        per_device, mesh=mesh, in_specs=in_specs, out_specs=P("grp", "ctx", None), check_vma=False
    )
```

```python
import functools

import jax
import jax.numpy as jnp
from jax import lax
from jax.experimental import pallas as pl
from jax.experimental.pallas import tpu as pltpu
from jax.sharding import PartitionSpec as P

score_factor = 0.0721688
NZ, NY = 16, 4
B, DL, DR, DN, DV = 8, 512, 64, 128, 128
SLOTS, TILE = 384, 128
NC = 4
BC = B // NC
ROWS = 2 * B
PART = DL // NC
QW = DL + 128
HEADS = NY * 2 * NZ
MESH = pl.DeviceIdType.MESH
FAR = (0, 4, -4, 8)
NEAR = (0, 2, 1, -1)
SLOT_OFFS = tuple((f + n + 7) % NZ - 7 for f in FAR for n in NEAR)
ORDER = tuple(sorted(range(1, NZ), key=lambda s: -abs(SLOT_OFFS[s])))
Y_OFFS = (2, 1, -1)
f32 = jnp.float32
bf16 = jnp.bfloat16


def kernel(
    qn_hbm, qr_hbm, wk_hbm, wv_hbm, codes_hbm, rope_hbm, scale_hbm, len_hbm, live_hbm, out_ref,
    qn, qr, wk, wv, codes, rope, scales, lens, live,
    qall, zf, obuf, rbuf, sbuf, srbuf, zr, zsend, zrecv, tsend, trecv,
    load_sem, fs, fr, ns, nr, ys, yr, hs, hr, ps, pr, pss, psr, os_, or_, oss, osr,
):
    me = lax.axis_index("ctx")
    z, y = me // NY, lax.rem(me, NY)

    def zid(k):
        return lax.rem(z + k + NZ, NZ)

    def yid(k):
        return lax.rem(y + k + NY, NY)

    def zdev(k):
        return {"ctx": zid(k) * NY + y}

    def ydev(k):
        return {"ctx": z * NY + yid(k)}

    def remote(src, dst, send, recv, device):
        return pltpu.make_async_remote_copy(
            src, dst, send, recv, device_id=device, device_id_type=MESH
        )

    pairs = (
        (qn_hbm, qn), (qr_hbm, qr), (wk_hbm, wk), (codes_hbm, codes), (rope_hbm, rope),
        (scale_hbm, scales), (len_hbm, lens), (live_hbm, live), (wv_hbm, wv),
    )

    def load(i):
        return pltpu.make_async_copy(pairs[i][0], pairs[i][1], load_sem.at[i])

    for i in range(len(pairs)):
        load(i).start()

    barrier = pltpu.get_barrier_semaphore()
    for k in SLOT_OFFS[1:]:
        pl.semaphore_signal(barrier, inc=1, device_id=zdev(k), device_id_type=MESH)
    for k in Y_OFFS:
        pl.semaphore_signal(barrier, inc=1, device_id=ydev(k), device_id_type=MESH)

    for i in range(3):
        load(i).wait()
    odd = lax.rem(lax.broadcasted_iota(jnp.int32, (ROWS, DL), 0), 2) == 1
    latent = jnp.where(
        odd,
        jnp.dot(qn[...], wk[1], preferred_element_type=f32),
        jnp.dot(qn[...], wk[0], preferred_element_type=f32),
    )
    qall[y, 0, 0, :, :DL] = latent.astype(bf16)
    qall[y, 0, 0, :, DL:] = jnp.concatenate(
        [qr[...].astype(f32), jnp.zeros((ROWS, 128 - DR), f32)], axis=1
    ).astype(bf16)

    pl.semaphore_wait(barrier, NZ - 1 + len(Y_OFFS))

    def far(f):
        return remote(qall.at[y, 0, 0], qall.at[y, f, 0], fs.at[f], fr.at[f], zdev(FAR[f]))

    def near(f, n):
        return remote(qall.at[y, f, 0], qall.at[y, f, n], ns.at[f, n], nr.at[f, n], zdev(NEAR[n]))

    def ycopy(f, i):
        mine = qall.at[y, f]
        return remote(mine, mine, ys.at[f, i], yr.at[f, i], ydev((1, -1)[i]))

    def hand(f, i):
        block = qall.at[yid((-1, 1)[i]), f, pl.ds((2, 0)[i], 2)]
        return remote(block, block, hs.at[f, i], hr.at[f, i], ydev((1, -1)[i]))

    def near_start(f):
        for n in range(1, 4):
            near(f, n).start()

    def y_start(f):
        for n in range(1, 4):
            near(f, n).wait_recv()
        for i in range(2):
            ycopy(f, i).start()

    def hand_start(f):
        for i in range(2):
            ycopy(f, i).wait_recv()
            hand(f, i).start()

    def widen(f):
        for i in range(2):
            hand(f, i).wait_recv()

        def store(v, carry):
            for n in range(4):
                block = qall[v, f, n].astype(f32)
                for j in range(QW // 128):
                    start = pl.multiple_of((v * NZ + f * 4 + n) * ROWS, ROWS)
                    zf[j, pl.ds(start, ROWS), :] = block[:, j * 128 : (j + 1) * 128]
            return carry

        lax.fori_loop(0, NY, store, 0)

    for f in (3, 1, 2):
        far(f).start()
    near_start(0)
    y_start(0)
    far(1).wait_recv()
    near_start(1)
    far(2).wait_recv()
    near_start(2)
    hand_start(0)
    far(3).wait_recv()
    near_start(3)
    y_start(1)
    y_start(2)
    hand_start(1)
    y_start(3)
    widen(0)
    hand_start(2)
    widen(1)
    hand_start(3)
    widen(2)
    for i in range(3, 8):
        load(i).wait()
    widen(3)

    def pcopy(c, i):
        return remote(
            obuf.at[c, yid(Y_OFFS[i])], rbuf.at[c, i], ps.at[c, i], pr.at[c, i], ydev(Y_OFFS[i])
        )

    def scopy(c, i):
        return remote(sbuf.at[c], srbuf.at[c, i], pss.at[c, i], psr.at[c, i], ydev(Y_OFFS[i]))

    lane = lax.broadcasted_iota(jnp.int32, (1, TILE), 1)
    eye = lax.broadcasted_iota(jnp.int32, (HEADS, HEADS), 0) == lax.broadcasted_iota(
        jnp.int32, (HEADS, HEADS), 1
    )

    def attend_one(c, r, carry):
        b = c * BC + r
        q = jnp.concatenate(
            [
                jnp.concatenate(
                    [
                        zf[j, pl.ds(v * NZ * ROWS + b * 2 + h, NZ, stride=ROWS), :].astype(bf16)
                        for v in range(NY)
                        for h in range(2)
                    ],
                    axis=0,
                )
                for j in range(QW // 128)
            ],
            axis=1,
        )
        codes_b = codes[b]
        part = lax.dot_general(
            q[:, :DL], codes_b, (((1,), (1,)), ((), ())), preferred_element_type=f32
        )
        turned = jnp.dot(q[:, DL : DL + DR], rope[b], preferred_element_type=f32)
        scale = scales[pl.ds(b, 1), :]
        length = lens[b]
        flags = []
        for t in range(SLOTS // TILE):
            limit = jnp.where(live[t, b] == 1, length - (me * SLOTS + t * TILE), 0)
            flags.append(jnp.where(lane < limit, f32(1.0), f32(0.0)))
        valid = jnp.concatenate(flags, axis=1) > 0.5
        scores = score_factor * (scale * part + turned)
        masked = jnp.where(valid, scores, f32(-1e30))
        top = jnp.max(masked, axis=1, keepdims=True)
        expo = jnp.where(valid, jnp.exp(masked - top), f32(0.0))
        total = jnp.sum(expo, axis=1, keepdims=True)
        probs = (expo * scale).astype(bf16)
        summed = jnp.dot(probs, codes_b, preferred_element_type=f32)
        for v in range(NY):
            obuf[c, v, r] = summed[v * 32 : v * 32 + 32].astype(bf16)
        sbuf[c, r, pl.ds(0, 1), :] = jnp.sum(jnp.where(eye, top, f32(0.0)), axis=0, keepdims=True)
        sbuf[c, r, pl.ds(1, 1), :] = jnp.sum(jnp.where(eye, total, f32(0.0)), axis=0, keepdims=True)
        return carry

    def attend(c):
        lax.fori_loop(0, BC, functools.partial(attend_one, c), 0)

    def pass_on(c):
        for i in range(3):
            scopy(c, i).start()
            pcopy(c, i).start()

    rows32 = lax.broadcasted_iota(jnp.int32, (32, 128), 0)
    lanes32 = lax.broadcasted_iota(jnp.int32, (32, 128), 1)
    pick = lanes32 == rows32 + y * 32
    lanes16 = lax.broadcasted_iota(jnp.int32, (NZ, 128), 1)

    def column(row):
        return jnp.sum(jnp.where(pick, row, f32(0.0)), axis=1, keepdims=True)

    def combine_one(c, r, stats):
        rows = [sbuf[c, r]] + [srbuf[c, i, r] for i in range(3)]
        tops = [column(t[0:1]) for t in rows]
        totals = [column(t[1:2]) for t in rows]
        top = functools.reduce(jnp.maximum, tops)
        factors = [jnp.exp(t - top) for t in tops]
        total = sum(f * t for f, t in zip(factors, totals))
        summed = factors[0] * obuf[c, y, r].astype(f32)
        for i in range(3):
            summed = summed + factors[i + 1] * rbuf[c, i, r].astype(f32)
        first, second = stats
        for h in range(2):
            mine = slice(h * 16, h * 16 + 16)
            for k in range(NC):
                for j in range(PART // 128):
                    lanes = k * PART + j * 128
                    zr[j, pl.ds(k * 2 * BC + r * 2 + h, 16, stride=16), :] = summed[mine, lanes : lanes + 128]
            first = jnp.where(lanes16 == (c * BC + r) * 2 + h, top[mine], first)
            second = jnp.where(lanes16 == (c * BC + r) * 2 + h, total[mine], second)
        return first, second

    def ocopy(c, s):
        return remote(zsend.at[c, s], zrecv.at[c, s], os_.at[c, s], or_.at[c, s], zdev(-SLOT_OFFS[s]))

    def tcopy(s):
        return remote(tsend.at[s], trecv.at[s], oss.at[s], osr.at[s], zdev(-SLOT_OFFS[s]))

    def combine(c, stats):
        for i in range(3):
            scopy(c, i).wait_recv()
            pcopy(c, i).wait_recv()
        stats = lax.fori_loop(0, BC, functools.partial(combine_one, c), stats)
        for s in range(NZ):
            for j in range(PART // 128):
                zsend[c, s, :, j * 128 : (j + 1) * 128] = zr[j, pl.ds(s * 16, 16), :].astype(bf16)
        for i in ORDER:
            ocopy(c, i).start()
        return stats

    def attend_all(c, carry):
        attend(c)
        pass_on(c)
        return carry

    lax.fori_loop(0, NC, attend_all, 0)
    blank = jnp.zeros((NZ, 128), f32)
    stats = lax.fori_loop(0, NC, combine, (blank, blank))
    for s in range(NZ):
        for p in range(2):
            tsend[s, p : p + 1, :] = stats[p][s : s + 1]
    for i in ORDER:
        tcopy(i).start()

    load(8).wait()
    odd16 = lax.rem(lax.broadcasted_iota(jnp.int32, (ROWS, DV), 0), 2) == 1
    for i in ORDER:
        tcopy(i).wait_recv()
    both = [tsend[0]] + [trecv[i] for i in range(1, NZ)]
    tops = jnp.concatenate([t[0:1] for t in both], axis=0)
    totals = jnp.concatenate([t[1:2] for t in both], axis=0)
    weights = jnp.exp(tops - jnp.max(tops, axis=0, keepdims=True))
    whole = jnp.sum(weights * totals, axis=0, keepdims=True)
    finished = []
    for c in range(NC):
        spot = lanes16 == c * 2 * BC + lax.rem(lax.broadcasted_iota(jnp.int32, (ROWS, 128), 0), 2 * BC)

        def spread_out(row, spot=spot):
            return jnp.sum(jnp.where(spot, row, f32(0.0)), axis=1, keepdims=True)

        summed = spread_out(weights[0:1]) * zsend[c, 0].astype(f32)
        for i in range(1, NZ):
            ocopy(c, i).wait_recv()
            summed = summed + spread_out(weights[i : i + 1]) * zrecv[c, i].astype(f32)
        summed = summed / spread_out(whole)
        finished.append(jnp.concatenate([summed[k * 2 * BC : (k + 1) * 2 * BC] for k in range(NC)], axis=1))
    latent_out = jnp.concatenate(finished, axis=0).astype(bf16)
    out_ref[...] = jnp.where(
        odd16,
        jnp.dot(latent_out, wv[1], preferred_element_type=f32),
        jnp.dot(latent_out, wv[0], preferred_element_type=f32),
    ).astype(bf16)

    for f in range(4):
        if f:
            far(f).wait_send()
        for n in range(1, 4):
            near(f, n).wait_send()
        for i in range(2):
            ycopy(f, i).wait_send()
            hand(f, i).wait_send()
    for i in ORDER:
        tcopy(i).wait_send()

    def drain(c, carry):
        for i in range(3):
            pcopy(c, i).wait_send()
            scopy(c, i).wait_send()
        for i in ORDER:
            ocopy(c, i).wait_send()
        return carry

    lax.fori_loop(0, NC, drain, 0)


def per_device(
    query_nope, query_rope, weight_key, weight_value, cache_codes, cache_rope, cache_scale, lengths, tile_live
):
    hbm = pl.BlockSpec(memory_space=pl.ANY)
    dma = pltpu.SemaphoreType.DMA
    vmem = pltpu.VMEM
    out = pl.pallas_call(
        kernel,
        out_shape=jax.ShapeDtypeStruct((ROWS, DV), bf16),
        in_specs=[hbm] * 9,
        out_specs=pl.BlockSpec(memory_space=pltpu.VMEM),
        scratch_shapes=[
            vmem((ROWS, DN), bf16),
            vmem((ROWS, DR), bf16),
            vmem((2, DN, DL), bf16),
            vmem((2, DL, DV), bf16),
            vmem((B, SLOTS, DL), bf16),
            vmem((B, DR, SLOTS), bf16),
            vmem((B, SLOTS), f32),
            pltpu.SMEM((B,), jnp.int32),
            pltpu.SMEM((SLOTS // TILE, B), jnp.int32),
            vmem((NY, 4, 4, ROWS, QW), bf16),
            vmem((QW // 128, NY * NZ * ROWS, 128), f32),
            vmem((NC, NY, BC, 32, DL), bf16),
            vmem((NC, 3, BC, 32, DL), bf16),
            vmem((NC, BC, 2, 128), f32),
            vmem((NC, 3, BC, 2, 128), f32),
            vmem((PART // 128, NZ * 16, 128), f32),
            vmem((NC, NZ, 16, PART), bf16),
            vmem((NC, NZ, 16, PART), bf16),
            vmem((NZ, 2, 128), f32),
            vmem((NZ, 2, 128), f32),
            dma((9,)),
            dma((4,)), dma((4,)),
            dma((4, 4)), dma((4, 4)),
            dma((4, 2)), dma((4, 2)),
            dma((4, 2)), dma((4, 2)),
            dma((NC, 3)), dma((NC, 3)),
            dma((NC, 3)), dma((NC, 3)),
            dma((NC, NZ)), dma((NC, NZ)),
            dma((NZ,)), dma((NZ,)),
        ],
        compiler_params=pltpu.CompilerParams(
            collective_id=0, has_side_effects=True, vmem_limit_bytes=60 * 1024 * 1024
        ),
        cost_estimate=pl.CostEstimate(flops=860_000_000, bytes_accessed=4_500_000, transcendentals=400_000),
        name="latent_decode",
    )(
        query_nope.reshape(ROWS, DN), query_rope.reshape(ROWS, DR), weight_key, weight_value, cache_codes,
        cache_rope.swapaxes(1, 2), cache_scale, lengths, tile_live.T,
    )
    return out.reshape(B, 2, DV)


def solution(mesh):
    in_specs = (
        P("grp", "ctx", None),
        P("grp", "ctx", None),
        P("ctx", None, None),
        P("ctx", None, None),
        P("grp", "ctx", None),
        P("grp", "ctx", None),
        P("grp", "ctx"),
        P("grp"),
        P("grp", "ctx"),
    )
    return jax.shard_map(
        per_device, mesh=mesh, in_specs=in_specs, out_specs=P("grp", "ctx", None), check_vma=False
    )
```

```python
import functools

import jax
import jax.numpy as jnp
from jax import lax
from jax.experimental import pallas as pl
from jax.experimental.pallas import tpu as pltpu
from jax.sharding import PartitionSpec as P

score_factor = 0.0721688
NZ, NY = 16, 4
B, DL, DR, DN, DV = 8, 512, 64, 128, 128
SLOTS, TILE = 384, 128
NC = 4
BC = B // NC
ROWS = 2 * B
PART = DL // NC
QW = DL + 128
HEADS = NY * 2 * NZ
MESH = pl.DeviceIdType.MESH
FAR = (0, 5, -5)
NEAR = (0, 1, -1, 2, -2, 3)
SIZE = (5, 6, 5)
FIRST = (0, 5, 11)
SLOT_PATHS = tuple((f, n) for f in range(3) for n in range(SIZE[f]))
Z_PARTNERS = (5, -5, 3, -3, 2, -2, 1, -1)


def place(f, n):
    return 3 * n + f if n < 5 else 15


Y_OFFS = (2, 1, -1)
f32 = jnp.float32
bf16 = jnp.bfloat16


def kernel(
    qn_hbm, qr_hbm, wk_hbm, wv_hbm, codes_hbm, rope_hbm, scale_hbm, len_hbm, live_hbm, out_ref,
    qn, qr, wk, wv, codes, rope, scales, lens, live,
    qall, zf, obuf, rbuf, sbuf, srbuf, zr, zsend, zrecv, tsend, trecv, mown, msend, mrecv, mtsend, mtrecv,
    load_sem, fs, fr, ns, nr, ys, yr, hs, hr, ps, pr, pss, psr, os_, or_, oss, osr, ms, mr, mss, msr,
):
    me = lax.axis_index("ctx")
    z, y = me // NY, lax.rem(me, NY)

    def zid(k):
        return lax.rem(z + k + NZ, NZ)

    def yid(k):
        return lax.rem(y + k + NY, NY)

    def zdev(k):
        return {"ctx": zid(k) * NY + y}

    def ydev(k):
        return {"ctx": z * NY + yid(k)}

    def remote(src, dst, send, recv, device):
        return pltpu.make_async_remote_copy(
            src, dst, send, recv, device_id=device, device_id_type=MESH
        )

    pairs = (
        (qn_hbm, qn), (qr_hbm, qr), (wk_hbm, wk), (codes_hbm, codes), (rope_hbm, rope),
        (scale_hbm, scales), (len_hbm, lens), (live_hbm, live), (wv_hbm, wv),
    )

    def load(i):
        return pltpu.make_async_copy(pairs[i][0], pairs[i][1], load_sem.at[i])

    for i in range(len(pairs)):
        load(i).start()

    barrier = pltpu.get_barrier_semaphore()
    for k in Z_PARTNERS:
        pl.semaphore_signal(barrier, inc=1, device_id=zdev(k), device_id_type=MESH)
    for k in Y_OFFS:
        pl.semaphore_signal(barrier, inc=1, device_id=ydev(k), device_id_type=MESH)

    for i in range(3):
        load(i).wait()
    odd = lax.rem(lax.broadcasted_iota(jnp.int32, (ROWS, DL), 0), 2) == 1
    latent = jnp.where(
        odd,
        jnp.dot(qn[...], wk[1], preferred_element_type=f32),
        jnp.dot(qn[...], wk[0], preferred_element_type=f32),
    )
    qall[y, 0, :, :DL] = latent.astype(bf16)
    qall[y, 0, :, DL:] = jnp.concatenate(
        [qr[...].astype(f32), jnp.zeros((ROWS, 128 - DR), f32)], axis=1
    ).astype(bf16)

    pl.semaphore_wait(barrier, len(Z_PARTNERS) + len(Y_OFFS))

    def far(f):
        return remote(qall.at[y, 0], qall.at[y, FIRST[f]], fs.at[f], fr.at[f], zdev(FAR[f]))

    def near(f, n):
        s = FIRST[f] + n
        return remote(qall.at[y, FIRST[f]], qall.at[y, s], ns.at[s], nr.at[s], zdev(NEAR[n]))

    def ycopy(f, i):
        mine = qall.at[y, pl.ds(FIRST[f], SIZE[f])]
        return remote(mine, mine, ys.at[f, i], yr.at[f, i], ydev((1, -1)[i]))

    def hand(f, i):
        part = (pl.ds(FIRST[f] + 3, SIZE[f] - 3), pl.ds(FIRST[f], 3))[i]
        block = qall.at[yid((-1, 1)[i]), part]
        return remote(block, block, hs.at[f, i], hr.at[f, i], ydev((1, -1)[i]))

    def near_start(f):
        for n in range(SIZE[f] - 1, 0, -1):
            near(f, n).start()

    def y_start(f):
        for n in range(1, SIZE[f]):
            near(f, n).wait_recv()
        for i in range(2):
            ycopy(f, i).start()

    def hand_start(f):
        for i in range(2):
            ycopy(f, i).wait_recv()
            hand(f, i).start()

    def widen(f):
        for i in range(2):
            hand(f, i).wait_recv()

        def store(v, carry):
            for n in range(SIZE[f]):
                block = qall[v, FIRST[f] + n].astype(f32)
                for j in range(QW // 128):
                    start = pl.multiple_of((v * NZ + FIRST[f] + n) * ROWS, ROWS)
                    zf[j, pl.ds(start, ROWS), :] = block[:, j * 128 : (j + 1) * 128]
            return carry

        lax.fori_loop(0, NY, store, 0)

    far(1).start()
    far(2).start()
    near_start(0)
    y_start(0)
    far(1).wait_recv()
    near_start(1)
    far(2).wait_recv()
    near_start(2)
    hand_start(0)
    y_start(1)
    y_start(2)
    widen(0)
    hand_start(1)
    hand_start(2)
    for i in range(3, 8):
        load(i).wait()
    widen(1)
    widen(2)

    def pcopy(c, i):
        return remote(
            obuf.at[c, yid(Y_OFFS[i])], rbuf.at[c, i], ps.at[c, i], pr.at[c, i], ydev(Y_OFFS[i])
        )

    def scopy(c, i):
        return remote(sbuf.at[c], srbuf.at[c, i], pss.at[c, i], psr.at[c, i], ydev(Y_OFFS[i]))

    lane = lax.broadcasted_iota(jnp.int32, (1, TILE), 1)
    eye = lax.broadcasted_iota(jnp.int32, (HEADS, HEADS), 0) == lax.broadcasted_iota(
        jnp.int32, (HEADS, HEADS), 1
    )

    def attend_one(c, r, carry):
        b = c * BC + r
        q = jnp.concatenate(
            [
                jnp.concatenate(
                    [
                        zf[j, pl.ds(v * NZ * ROWS + b * 2 + h, NZ, stride=ROWS), :].astype(bf16)
                        for v in range(NY)
                        for h in range(2)
                    ],
                    axis=0,
                )
                for j in range(QW // 128)
            ],
            axis=1,
        )
        codes_b = codes[b]
        part = lax.dot_general(
            q[:, :DL], codes_b, (((1,), (1,)), ((), ())), preferred_element_type=f32
        )
        turned = jnp.dot(q[:, DL : DL + DR], rope[b], preferred_element_type=f32)
        scale = scales[pl.ds(b, 1), :]
        length = lens[b]
        flags = []
        for t in range(SLOTS // TILE):
            limit = jnp.where(live[t, b] == 1, length - (me * SLOTS + t * TILE), 0)
            flags.append(jnp.where(lane < limit, f32(1.0), f32(0.0)))
        valid = jnp.concatenate(flags, axis=1) > 0.5
        scores = score_factor * (scale * part + turned)
        masked = jnp.where(valid, scores, f32(-1e30))
        top = jnp.max(masked, axis=1, keepdims=True)
        expo = jnp.where(valid, jnp.exp(masked - top), f32(0.0))
        total = jnp.sum(expo, axis=1, keepdims=True)
        probs = (expo * scale).astype(bf16)
        summed = jnp.dot(probs, codes_b, preferred_element_type=f32)
        for v in range(NY):
            obuf[c, v, r] = summed[v * 32 : v * 32 + 32].astype(bf16)
        sbuf[c, r, pl.ds(0, 1), :] = jnp.sum(jnp.where(eye, top, f32(0.0)), axis=0, keepdims=True)
        sbuf[c, r, pl.ds(1, 1), :] = jnp.sum(jnp.where(eye, total, f32(0.0)), axis=0, keepdims=True)
        return carry

    def attend(c):
        lax.fori_loop(0, BC, functools.partial(attend_one, c), 0)

    def pass_on(c):
        for i in range(3):
            scopy(c, i).start()
            pcopy(c, i).start()

    rows32 = lax.broadcasted_iota(jnp.int32, (32, 128), 0)
    lanes32 = lax.broadcasted_iota(jnp.int32, (32, 128), 1)
    pick = lanes32 == rows32 + y * 32
    lanes16 = lax.broadcasted_iota(jnp.int32, (NZ, 128), 1)

    def column(row):
        return jnp.sum(jnp.where(pick, row, f32(0.0)), axis=1, keepdims=True)

    def combine_one(c, r, stats):
        rows = [sbuf[c, r]] + [srbuf[c, i, r] for i in range(3)]
        tops = [column(t[0:1]) for t in rows]
        totals = [column(t[1:2]) for t in rows]
        top = functools.reduce(jnp.maximum, tops)
        factors = [jnp.exp(t - top) for t in tops]
        total = sum(f * t for f, t in zip(factors, totals))
        summed = factors[0] * obuf[c, y, r].astype(f32)
        for i in range(3):
            summed = summed + factors[i + 1] * rbuf[c, i, r].astype(f32)
        first, second = stats
        for h in range(2):
            mine = slice(h * 16, h * 16 + 16)
            for k in range(NC):
                zr[pl.ds(k * 2 * BC + r * 2 + h, 16, stride=16), :] = summed[mine, k * PART : (k + 1) * PART]
            first = jnp.where(lanes16 == r * 2 + h, top[mine], first)
            second = jnp.where(lanes16 == r * 2 + h, total[mine], second)
        return first, second

    def group(n):
        return pl.ds(3 * n, 3) if n < 5 else pl.ds(15, 1)

    def ocopy(c, n):
        part = group(n)
        return remote(zsend.at[c, part], zrecv.at[c, part], os_.at[c, n], or_.at[c, n], zdev(-NEAR[n]))

    def tcopy(c, n):
        part = group(n)
        return remote(tsend.at[c, part], trecv.at[c, part], oss.at[c, n], osr.at[c, n], zdev(-NEAR[n]))

    def mcopy(c, f):
        return remote(msend.at[c, f], mrecv.at[c, f], ms.at[c, f], mr.at[c, f], zdev(-FAR[f]))

    def mtcopy(c, f):
        return remote(mtsend.at[c, f], mtrecv.at[c, f], mss.at[c, f], msr.at[c, f], zdev(-FAR[f]))

    def combine(c, carry):
        for i in range(3):
            scopy(c, i).wait_recv()
            pcopy(c, i).wait_recv()
        blank = jnp.zeros((NZ, 128), f32)
        first, second = lax.fori_loop(0, BC, functools.partial(combine_one, c), (blank, blank))
        for s, path in enumerate(SLOT_PATHS):
            p = place(*path)
            zsend[c, p] = zr[pl.ds(s * 16, 16), :].astype(bf16)
            tsend[c, p, 0:1, :] = first[s : s + 1]
            tsend[c, p, 1:2, :] = second[s : s + 1]
        for n in range(5, 0, -1):
            tcopy(c, n).start()
            ocopy(c, n).start()
        return carry

    spot = lanes16 == lax.rem(lax.broadcasted_iota(jnp.int32, (ROWS, 128), 0), 2 * BC)

    def spread_out(row):
        return jnp.sum(jnp.where(spot, row, f32(0.0)), axis=1, keepdims=True)

    def merge(stats, blocks):
        tops = [t[0:1] for t in stats]
        top = functools.reduce(jnp.maximum, tops)
        weights = [jnp.exp(t - top) for t in tops]
        whole = sum(w * t[1:2] for w, t in zip(weights, stats))
        return top, whole, sum(spread_out(w) * block.astype(f32) for w, block in zip(weights, blocks))

    def middle(c, carry):
        for n in range(1, 6):
            tcopy(c, n).wait_recv()
            ocopy(c, n).wait_recv()
        for f in (1, 2, 0):
            places = [place(f, n) for n in range(1, SIZE[f])]
            top, whole, summed = merge(
                [tsend[c, f]] + [trecv[c, p] for p in places],
                [zsend[c, f]] + [zrecv[c, p] for p in places],
            )
            mtsend[c, f, 0:1, :] = top
            mtsend[c, f, 1:2, :] = whole
            if f == 0:
                mown[c] = summed
            else:
                msend[c, f] = summed.astype(bf16)
                mtcopy(c, f).start()
                mcopy(c, f).start()
        return carry

    def attend_all(c, carry):
        attend(c)
        pass_on(c)
        return carry

    lax.fori_loop(0, NC, attend_all, 0)
    lax.fori_loop(0, NC, combine, 0)
    lax.fori_loop(0, NC, middle, 0)

    load(8).wait()
    odd16 = lax.rem(lax.broadcasted_iota(jnp.int32, (ROWS, DV), 0), 2) == 1
    finished = []
    for c in range(NC):
        for f in (1, 2):
            mtcopy(c, f).wait_recv()
            mcopy(c, f).wait_recv()
        _, whole, summed = merge(
            [mtsend[c, 0], mtrecv[c, 1], mtrecv[c, 2]], [mown[c], mrecv[c, 1], mrecv[c, 2]]
        )
        summed = summed / spread_out(whole)
        finished.append(
            jnp.concatenate([summed[k * 2 * BC : (k + 1) * 2 * BC] for k in range(NC)], axis=1)
        )
    latent_out = jnp.concatenate(finished, axis=0).astype(bf16)
    out_ref[...] = jnp.where(
        odd16,
        jnp.dot(latent_out, wv[1], preferred_element_type=f32),
        jnp.dot(latent_out, wv[0], preferred_element_type=f32),
    ).astype(bf16)

    for f in range(3):
        if f:
            far(f).wait_send()
        for n in range(1, SIZE[f]):
            near(f, n).wait_send()
        for i in range(2):
            ycopy(f, i).wait_send()
            hand(f, i).wait_send()

    def drain(c, carry):
        for i in range(3):
            pcopy(c, i).wait_send()
            scopy(c, i).wait_send()
        for n in range(1, 6):
            tcopy(c, n).wait_send()
            ocopy(c, n).wait_send()
        for f in (1, 2):
            mtcopy(c, f).wait_send()
            mcopy(c, f).wait_send()
        return carry

    lax.fori_loop(0, NC, drain, 0)


def per_device(
    query_nope, query_rope, weight_key, weight_value, cache_codes, cache_rope, cache_scale, lengths, tile_live
):
    hbm = pl.BlockSpec(memory_space=pl.ANY)
    dma = pltpu.SemaphoreType.DMA
    vmem = pltpu.VMEM
    out = pl.pallas_call(
        kernel,
        out_shape=jax.ShapeDtypeStruct((ROWS, DV), bf16),
        in_specs=[hbm] * 9,
        out_specs=pl.BlockSpec(memory_space=pltpu.VMEM),
        scratch_shapes=[
            vmem((ROWS, DN), bf16),
            vmem((ROWS, DR), bf16),
            vmem((2, DN, DL), bf16),
            vmem((2, DL, DV), bf16),
            vmem((B, SLOTS, DL), bf16),
            vmem((B, DR, SLOTS), bf16),
            vmem((B, SLOTS), f32),
            pltpu.SMEM((B,), jnp.int32),
            pltpu.SMEM((SLOTS // TILE, B), jnp.int32),
            vmem((NY, NZ, ROWS, QW), bf16),
            vmem((QW // 128, NY * NZ * ROWS, 128), f32),
            vmem((NC, NY, BC, 32, DL), bf16),
            vmem((NC, 3, BC, 32, DL), bf16),
            vmem((NC, BC, 2, 128), f32),
            vmem((NC, 3, BC, 2, 128), f32),
            vmem((NZ * 16, PART), f32),
            vmem((NC, NZ, 16, PART), bf16),
            vmem((NC, NZ, 16, PART), bf16),
            vmem((NC, NZ, 2, 128), f32),
            vmem((NC, NZ, 2, 128), f32),
            vmem((NC, 16, PART), f32),
            vmem((NC, 3, 16, PART), bf16),
            vmem((NC, 3, 16, PART), bf16),
            vmem((NC, 3, 2, 128), f32),
            vmem((NC, 3, 2, 128), f32),
            dma((9,)),
            dma((3,)), dma((3,)),
            dma((NZ,)), dma((NZ,)),
            dma((3, 2)), dma((3, 2)),
            dma((3, 2)), dma((3, 2)),
            dma((NC, 3)), dma((NC, 3)),
            dma((NC, 3)), dma((NC, 3)),
            dma((NC, 6)), dma((NC, 6)),
            dma((NC, 6)), dma((NC, 6)),
            dma((NC, 3)), dma((NC, 3)),
            dma((NC, 3)), dma((NC, 3)),
        ],
        compiler_params=pltpu.CompilerParams(
            collective_id=0, has_side_effects=True, vmem_limit_bytes=60 * 1024 * 1024
        ),
        cost_estimate=pl.CostEstimate(flops=860_000_000, bytes_accessed=4_500_000, transcendentals=400_000),
        name="latent_decode",
    )(
        query_nope.reshape(ROWS, DN), query_rope.reshape(ROWS, DR), weight_key, weight_value, cache_codes,
        cache_rope.swapaxes(1, 2), cache_scale, lengths, tile_live.T,
    )
    return out.reshape(B, 2, DV)


def solution(mesh):
    in_specs = (
        P("grp", "ctx", None),
        P("grp", "ctx", None),
        P("ctx", None, None),
        P("ctx", None, None),
        P("grp", "ctx", None),
        P("grp", "ctx", None),
        P("grp", "ctx"),
        P("grp"),
        P("grp", "ctx"),
    )
    return jax.shard_map(
        per_device, mesh=mesh, in_specs=in_specs, out_specs=P("grp", "ctx", None), check_vma=False
    )
```

```python
import functools

import jax
import jax.numpy as jnp
from jax import lax
from jax.experimental import pallas as pl
from jax.experimental.pallas import tpu as pltpu
from jax.sharding import PartitionSpec as P

score_factor = 0.0721688
NZ, NY = 16, 4
B, DL, DR, DN, DV = 8, 512, 64, 128, 128
SLOTS, TILE = 384, 128
NB = 1
NC = 4
BC = B // NC
ROWS = 2 * B
PART = DL // NC
QW = DL + 128
HEADS = NY * 2 * NZ
MESH = pl.DeviceIdType.MESH
FAR = (0, 5, -5)
NEAR = (0, 1, -1, 2, -2, 3)
SIZE = (5, 6, 5)
FIRST = (0, 5, 11)
PIECES = ((0, 1), (1, 4), (5, 1), (6, 5), (11, 1), (12, 4))
HANDED = 3
Z_PARTNERS = (5, -5, 3, -3, 2, -2, 1, -1)


def place(f, n):
    return 3 * n + f if n < 5 else 15


Y_OFFS = (2, 1, -1)
f32 = jnp.float32
bf16 = jnp.bfloat16


PLACES = tuple(place(f, n) for f in range(3) for n in range(SIZE[f]))


def kernel(
    qn_hbm, qr_hbm, wk_hbm, wv_hbm, codes_hbm, rope_hbm, scale_hbm, len_hbm, live_hbm, out_ref,
    qn, qr, wk, wv, codes, rope, scales, lens, live,
    qall, zf, obuf, rbuf, sbuf, srbuf, zr, zsend, zrecv, tsend, trecv, mown, msend, mrecv, mtsend, mtrecv,
    zb, bsend, brecv, tb, trb, ysend, yrecv, yt, ytr,
    load_sem, fs, fr, ns, nr, ys, yr, hs, hr, ps, pr, pss, psr, os_, or_, oss, osr, ms, mr, mss, msr, bs, br, bts, btr, es, er, ets, etr,
):
    me = lax.axis_index("ctx")
    z, y = me // NY, lax.rem(me, NY)

    def zid(k):
        return lax.rem(z + k + NZ, NZ)

    def yid(k):
        return lax.rem(y + k + NY, NY)

    def zdev(k):
        return {"ctx": zid(k) * NY + y}

    def ydev(k):
        return {"ctx": z * NY + yid(k)}

    def remote(src, dst, send, recv, device):
        return pltpu.make_async_remote_copy(
            src, dst, send, recv, device_id=device, device_id_type=MESH
        )

    pairs = (
        (qn_hbm, qn), (qr_hbm, qr), (wk_hbm, wk), (codes_hbm, codes), (rope_hbm, rope),
        (scale_hbm, scales), (len_hbm, lens), (live_hbm, live), (wv_hbm, wv),
    )

    def load(i):
        return pltpu.make_async_copy(pairs[i][0], pairs[i][1], load_sem.at[i])

    for i in range(len(pairs)):
        load(i).start()

    barrier = pltpu.get_barrier_semaphore()
    for k in Z_PARTNERS:
        pl.semaphore_signal(barrier, inc=1, device_id=zdev(k), device_id_type=MESH)
    for k in Y_OFFS:
        pl.semaphore_signal(barrier, inc=1, device_id=ydev(k), device_id_type=MESH)

    for i in range(3):
        load(i).wait()
    odd = lax.rem(lax.broadcasted_iota(jnp.int32, (ROWS, DL), 0), 2) == 1
    latent = jnp.where(
        odd,
        jnp.dot(qn[...], wk[1], preferred_element_type=f32),
        jnp.dot(qn[...], wk[0], preferred_element_type=f32),
    )
    qall[y, 0, :, :DL] = latent.astype(bf16)
    qall[y, 0, :, DL:] = jnp.concatenate(
        [qr[...].astype(f32), jnp.zeros((ROWS, 128 - DR), f32)], axis=1
    ).astype(bf16)

    pl.semaphore_wait(barrier, len(Z_PARTNERS) + len(Y_OFFS))

    def far(f):
        return remote(qall.at[y, 0], qall.at[y, FIRST[f]], fs.at[f], fr.at[f], zdev(FAR[f]))

    def near(f, n):
        s = FIRST[f] + n
        return remote(qall.at[y, FIRST[f]], qall.at[y, s], ns.at[s], nr.at[s], zdev(NEAR[n]))

    def ycopy(p, i):
        mine = qall.at[y, pl.ds(*PIECES[p])]
        return remote(mine, mine, ys.at[p, i], yr.at[p, i], ydev((1, -1, 2)[i]))

    def partners(p):
        return range(2 if p == HANDED else 3)

    def hand(i):
        start, size = PIECES[HANDED]
        part = (pl.ds(start + 3, size - 3), pl.ds(start, 3))[i]
        block = qall.at[yid((-1, 1)[i]), part]
        return remote(block, block, hs.at[i], hr.at[i], ydev((1, -1)[i]))

    def near_start(f):
        for n in range(SIZE[f] - 1, 0, -1):
            near(f, n).start()

    def near_wait(f):
        for n in range(1, SIZE[f]):
            near(f, n).wait_recv()

    def y_start(p):
        for i in partners(p):
            ycopy(p, i).start()

    def widen(p):
        if p == HANDED:
            for i in range(2):
                hand(i).wait_recv()
        else:
            for i in range(3):
                ycopy(p, i).wait_recv()
        first, size = PIECES[p]

        def store(v, carry):
            for n in range(size):
                block = qall[v, first + n].astype(f32)
                for j in range(QW // 128):
                    start = pl.multiple_of((v * NZ + PLACES[first + n]) * ROWS, ROWS)
                    zf[j, pl.ds(start, ROWS), :] = block[:, j * 128 : (j + 1) * 128]
            return carry

        lax.fori_loop(0, NY, store, 0)

    far(1).start()
    far(2).start()
    near_start(0)
    y_start(0)
    near_wait(0)
    y_start(1)
    far(1).wait_recv()
    near_start(1)
    y_start(2)
    far(2).wait_recv()
    near_start(2)
    y_start(4)
    near_wait(1)
    y_start(3)
    near_wait(2)
    y_start(5)
    for p in (0, 1, 2, 4):
        widen(p)
    for i in range(2):
        ycopy(HANDED, i).wait_recv()
        hand(i).start()
    for i in range(3, 8):
        load(i).wait()
    widen(5)
    widen(3)

    def pcopy(c, r, i):
        return remote(
            obuf.at[c, yid(Y_OFFS[i]), r], rbuf.at[c, i, r], ps.at[c, r, i], pr.at[c, r, i], ydev(Y_OFFS[i])
        )

    def scopy(c, i):
        return remote(sbuf.at[c], srbuf.at[c, i], pss.at[c, i], psr.at[c, i], ydev(Y_OFFS[i]))

    lane = lax.broadcasted_iota(jnp.int32, (1, TILE), 1)
    lanes16 = lax.broadcasted_iota(jnp.int32, (NZ, 128), 1)
    eye = lax.broadcasted_iota(jnp.int32, (HEADS, HEADS), 0) == lax.broadcasted_iota(
        jnp.int32, (HEADS, HEADS), 1
    )

    def attend_one(c, r):
        b = c * BC + r
        q = jnp.concatenate(
            [
                jnp.concatenate(
                    [
                        zf[j, pl.ds(v * NZ * ROWS + b * 2 + h, NZ, stride=ROWS), :].astype(bf16)
                        for v in range(NY)
                        for h in range(2)
                    ],
                    axis=0,
                )
                for j in range(QW // 128)
            ],
            axis=1,
        )
        codes_b = codes[b]
        part = lax.dot_general(
            q[:, :DL], codes_b, (((1,), (1,)), ((), ())), preferred_element_type=f32
        )
        turned = jnp.dot(q[:, DL : DL + DR], rope[b], preferred_element_type=f32)
        scale = scales[pl.ds(b, 1), :]
        length = lens[b]
        flags = []
        for t in range(SLOTS // TILE):
            limit = jnp.where(live[t, b] == 1, length - (me * SLOTS + t * TILE), 0)
            flags.append(jnp.where(lane < limit, f32(1.0), f32(0.0)))
        valid = jnp.concatenate(flags, axis=1) > 0.5
        scores = score_factor * (scale * part + turned)
        masked = jnp.where(valid, scores, f32(-1e30))
        top = jnp.max(masked, axis=1, keepdims=True)
        expo = jnp.where(valid, jnp.exp(masked - top), f32(0.0))
        total = jnp.sum(expo, axis=1, keepdims=True)
        probs = (expo * scale).astype(bf16)
        summed = jnp.dot(probs, codes_b, preferred_element_type=f32)
        return top, total, summed

    def attend_y(c, r, carry):
        top, total, summed = attend_one(c, r)
        for v in range(NY):
            obuf[c, v, r] = summed[v * 32 : v * 32 + 32].astype(bf16)
        for i in range(3):
            pcopy(c, r, i).start()
        sbuf[c, r, pl.ds(0, 1), :] = jnp.sum(jnp.where(eye, top, f32(0.0)), axis=0, keepdims=True)
        sbuf[c, r, pl.ds(1, 1), :] = jnp.sum(jnp.where(eye, total, f32(0.0)), axis=0, keepdims=True)
        return carry

    def attend_z(c, r, stats):
        found = attend_one(c, r)
        for v in range(NY):
            for h in range(2):
                mine = slice(v * 32 + h * 16, v * 32 + h * 16 + 16)
                for k in range(NC):
                    zb[pl.ds(v * 256 + k * 2 * BC + r * 2 + h, 16, stride=16), :] = found[2][
                        mine, k * PART : (k + 1) * PART
                    ]
                stats = tuple(
                    jnp.where(lanes16 == r * 2 + h, found[i % 2][mine], old) if i // 2 == v else old
                    for i, old in enumerate(stats)
                )
        return stats

    def pass_on(c):
        for i in range(3):
            scopy(c, i).start()

    rows32 = lax.broadcasted_iota(jnp.int32, (32, 128), 0)
    lanes32 = lax.broadcasted_iota(jnp.int32, (32, 128), 1)
    pick = lanes32 == rows32 + y * 32

    def column(row):
        return jnp.sum(jnp.where(pick, row, f32(0.0)), axis=1, keepdims=True)

    def combine_one(c, r, stats):
        rows = [sbuf[c, r]] + [srbuf[c, i, r] for i in range(3)]
        tops = [column(t[0:1]) for t in rows]
        totals = [column(t[1:2]) for t in rows]
        top = functools.reduce(jnp.maximum, tops)
        factors = [jnp.exp(t - top) for t in tops]
        total = sum(f * t for f, t in zip(factors, totals))
        summed = factors[0] * obuf[c, y, r].astype(f32)
        for i in range(3):
            summed = summed + factors[i + 1] * rbuf[c, i, r].astype(f32)
        first, second = stats
        for h in range(2):
            mine = slice(h * 16, h * 16 + 16)
            for k in range(NC):
                zr[pl.ds(k * 2 * BC + r * 2 + h, 16, stride=16), :] = summed[mine, k * PART : (k + 1) * PART]
            first = jnp.where(lanes16 == r * 2 + h, top[mine], first)
            second = jnp.where(lanes16 == r * 2 + h, total[mine], second)
        return first, second

    def group(n):
        return pl.ds(3 * n, 3) if n < 5 else pl.ds(15, 1)

    def ocopy(c, n):
        part = group(n)
        return remote(zsend.at[c, part], zrecv.at[c, part], os_.at[c, n], or_.at[c, n], zdev(-NEAR[n]))

    def tcopy(c, n):
        part = group(n)
        return remote(tsend.at[c, part], trecv.at[c, part], oss.at[c, n], osr.at[c, n], zdev(-NEAR[n]))

    def mcopy(c, f):
        return remote(msend.at[c, f], mrecv.at[c, f], ms.at[c, f], mr.at[c, f], zdev(-FAR[f]))

    def mtcopy(c, f):
        return remote(mtsend.at[c, f], mtrecv.at[c, f], mss.at[c, f], msr.at[c, f], zdev(-FAR[f]))

    def combine(c, carry):
        for i in range(3):
            scopy(c, i).wait_recv()
            for r in range(BC):
                pcopy(c, r, i).wait_recv()
        blank = jnp.zeros((NZ, 128), f32)
        first, second = lax.fori_loop(0, BC, functools.partial(combine_one, c), (blank, blank))
        for p in range(NZ):
            zsend[c, p] = zr[pl.ds(p * 16, 16), :].astype(bf16)
            tsend[c, p, 0:1, :] = first[p : p + 1]
            tsend[c, p, 1:2, :] = second[p : p + 1]
        for n in range(5, 0, -1):
            tcopy(c, n).start()
            ocopy(c, n).start()
        return carry

    spot = lanes16 == lax.rem(lax.broadcasted_iota(jnp.int32, (ROWS, 128), 0), 2 * BC)

    def spread_out(row):
        return jnp.sum(jnp.where(spot, row, f32(0.0)), axis=1, keepdims=True)

    def merge_rows(own, others, blocks):
        tops = [own[0]] + [t[0] for t in others]
        totals = [own[1]] + [t[1] for t in others]
        top = functools.reduce(jnp.maximum, tops)
        weights = [jnp.exp(t - top) for t in tops]
        whole = sum(w * t for w, t in zip(weights, totals))
        return top, whole, sum(spread_out(w) * block.astype(f32) for w, block in zip(weights, blocks))

    def merge(stats, blocks):
        rows = [(t[0:1], t[1:2]) for t in stats]
        return merge_rows(rows[0], rows[1:], blocks)

    def forward(c, f, top, whole, summed):
        mtsend[c, f, 0:1, :] = top
        mtsend[c, f, 1:2, :] = whole
        if f == 0:
            mown[c] = summed
        else:
            msend[c, f] = summed.astype(bf16)
            mtcopy(c, f).start()
            mcopy(c, f).start()

    def middle(c, carry):
        for n in range(1, 6):
            tcopy(c, n).wait_recv()
            ocopy(c, n).wait_recv()
        for f in (1, 2, 0):
            places = [place(f, n) for n in range(1, SIZE[f])]
            merged = merge(
                [tsend[c, f]] + [trecv[c, p] for p in places],
                [zsend[c, f]] + [zrecv[c, p] for p in places],
            )
            forward(c, f, *merged)
        return carry

    def bcopy(c, n):
        part = group(n)
        return remote(bsend.at[c, part], brecv.at[c, part], bs.at[c, n], br.at[c, n], zdev(-NEAR[n]))

    def btcopy(c, n):
        part = pl.ds(24 * n, 24) if n < 5 else pl.ds(120, 8)
        return remote(tb.at[c, part], trb.at[c, part], bts.at[c, n], btr.at[c, n], zdev(-NEAR[n]))

    def ecopy(c, i):
        return remote(
            ysend.at[c, yid(Y_OFFS[i])], yrecv.at[c, i], es.at[c, i], er.at[c, i], ydev(Y_OFFS[i])
        )

    def etcopy(c, i):
        return remote(yt.at[c, yid(Y_OFFS[i])], ytr.at[c, i], ets.at[c, i], etr.at[c, i], ydev(Y_OFFS[i]))

    def z_first(c, carry):
        stats = (jnp.zeros((NZ, 128), f32),) * (2 * NY)
        stats = lax.fori_loop(0, BC, functools.partial(attend_z, c), stats)
        for i in range(2 * NY):
            tb[c, pl.ds(i, NZ, stride=8), :] = stats[i]

        def pack(v, carry):
            for p in range(NZ):
                bsend[c, p, v] = zb[pl.ds(pl.multiple_of(v * 256 + p * 16, 16), 16), :].astype(bf16)
            return carry

        lax.fori_loop(0, NY, pack, 0)
        for n in range(5, 0, -1):
            btcopy(c, n).start()
            bcopy(c, n).start()
        return carry

    def z_middle(c, carry):
        for n in range(1, 6):
            btcopy(c, n).wait_recv()
            bcopy(c, n).wait_recv()

        def one(v, carry):
            for f in range(3):
                places = [place(f, n) for n in range(1, SIZE[f])]
                top, whole, summed = merge_rows(
                    [tb[c, pl.ds(f * 8 + v * 2 + m, 1), :] for m in range(2)],
                    [[trb[c, pl.ds(p * 8 + v * 2 + m, 1), :] for m in range(2)] for p in places],
                    [bsend[c, f, v]] + [brecv[c, p, v] for p in places],
                )
                ysend[c, v, f] = summed.astype(bf16)
                yt[c, v, f * 2 : f * 2 + 1, :] = top
                yt[c, v, f * 2 + 1 : f * 2 + 2, :] = whole
            return carry

        lax.fori_loop(0, NY, one, 0)
        for i in range(3):
            etcopy(c, i).start()
            ecopy(c, i).start()
        return carry

    def z_last(c, carry):
        for i in range(3):
            etcopy(c, i).wait_recv()
            ecopy(c, i).wait_recv()
        for f in (1, 2, 0):
            merged = merge_rows(
                [yt[c, y, f * 2 + m : f * 2 + m + 1, :] for m in range(2)],
                [[ytr[c, i, f * 2 + m : f * 2 + m + 1, :] for m in range(2)] for i in range(3)],
                [ysend[c, y, f]] + [yrecv[c, i, f] for i in range(3)],
            )
            forward(c, f, *merged)
        return carry

    def y_first(c, carry):
        lax.fori_loop(0, BC, functools.partial(attend_y, c), 0)
        pass_on(c)
        return carry

    lax.fori_loop(0, NB, z_first, 0)
    lax.fori_loop(NB, NC, y_first, 0)
    lax.fori_loop(0, NB, z_middle, 0)
    lax.fori_loop(NB, NC, combine, 0)
    lax.fori_loop(0, NB, z_last, 0)
    lax.fori_loop(NB, NC, middle, 0)

    load(8).wait()
    odd16 = lax.rem(lax.broadcasted_iota(jnp.int32, (ROWS, DV), 0), 2) == 1
    finished = []
    for c in range(NC):
        for f in (1, 2):
            mtcopy(c, f).wait_recv()
            mcopy(c, f).wait_recv()
        _, whole, summed = merge(
            [mtsend[c, 0], mtrecv[c, 1], mtrecv[c, 2]], [mown[c], mrecv[c, 1], mrecv[c, 2]]
        )
        summed = summed / spread_out(whole)
        finished.append(
            jnp.concatenate([summed[k * 2 * BC : (k + 1) * 2 * BC] for k in range(NC)], axis=1)
        )
    latent_out = jnp.concatenate(finished, axis=0).astype(bf16)
    out_ref[...] = jnp.where(
        odd16,
        jnp.dot(latent_out, wv[1], preferred_element_type=f32),
        jnp.dot(latent_out, wv[0], preferred_element_type=f32),
    ).astype(bf16)

    for f in range(3):
        if f:
            far(f).wait_send()
        for n in range(1, SIZE[f]):
            near(f, n).wait_send()
    for p in range(len(PIECES)):
        for i in partners(p):
            ycopy(p, i).wait_send()
    for i in range(2):
        hand(i).wait_send()

    def drain_y(c, carry):
        for i in range(3):
            for r in range(BC):
                pcopy(c, r, i).wait_send()
            scopy(c, i).wait_send()
        for n in range(1, 6):
            tcopy(c, n).wait_send()
            ocopy(c, n).wait_send()
        return carry

    def drain_z(c, carry):
        for n in range(1, 6):
            btcopy(c, n).wait_send()
            bcopy(c, n).wait_send()
        for i in range(3):
            etcopy(c, i).wait_send()
            ecopy(c, i).wait_send()
        return carry

    def drain(c, carry):
        for f in (1, 2):
            mtcopy(c, f).wait_send()
            mcopy(c, f).wait_send()
        return carry

    lax.fori_loop(0, NB, drain_z, 0)
    lax.fori_loop(NB, NC, drain_y, 0)
    lax.fori_loop(0, NC, drain, 0)


def per_device(
    query_nope, query_rope, weight_key, weight_value, cache_codes, cache_rope, cache_scale, lengths, tile_live
):
    hbm = pl.BlockSpec(memory_space=pl.ANY)
    dma = pltpu.SemaphoreType.DMA
    vmem = pltpu.VMEM
    out = pl.pallas_call(
        kernel,
        out_shape=jax.ShapeDtypeStruct((ROWS, DV), bf16),
        in_specs=[hbm] * 9,
        out_specs=pl.BlockSpec(memory_space=pltpu.VMEM),
        scratch_shapes=[
            vmem((ROWS, DN), bf16),
            vmem((ROWS, DR), bf16),
            vmem((2, DN, DL), bf16),
            vmem((2, DL, DV), bf16),
            vmem((B, SLOTS, DL), bf16),
            vmem((B, DR, SLOTS), bf16),
            vmem((B, SLOTS), f32),
            pltpu.SMEM((B,), jnp.int32),
            pltpu.SMEM((SLOTS // TILE, B), jnp.int32),
            vmem((NY, NZ, ROWS, QW), bf16),
            vmem((QW // 128, NY * NZ * ROWS, 128), f32),
            vmem((NC, NY, BC, 32, DL), bf16),
            vmem((NC, 3, BC, 32, DL), bf16),
            vmem((NC, BC, 2, 128), f32),
            vmem((NC, 3, BC, 2, 128), f32),
            vmem((NZ * 16, PART), f32),
            vmem((NC, NZ, 16, PART), bf16),
            vmem((NC, NZ, 16, PART), bf16),
            vmem((NC, NZ, 2, 128), f32),
            vmem((NC, NZ, 2, 128), f32),
            vmem((NC, 16, PART), f32),
            vmem((NC, 3, 16, PART), bf16),
            vmem((NC, 3, 16, PART), bf16),
            vmem((NC, 3, 2, 128), f32),
            vmem((NC, 3, 2, 128), f32),
            vmem((NY * NZ * 16, PART), f32),
            vmem((NB, NZ, NY, 16, PART), bf16),
            vmem((NB, NZ, NY, 16, PART), bf16),
            vmem((NB, NZ * 8, 128), f32),
            vmem((NB, NZ * 8, 128), f32),
            vmem((NB, NY, 3, 16, PART), bf16),
            vmem((NB, 3, 3, 16, PART), bf16),
            vmem((NB, NY, 8, 128), f32),
            vmem((NB, 3, 8, 128), f32),
            dma((9,)),
            dma((3,)), dma((3,)),
            dma((NZ,)), dma((NZ,)),
            dma((len(PIECES), 3)), dma((len(PIECES), 3)),
            dma((2,)), dma((2,)),
            dma((NC, BC, 3)), dma((NC, BC, 3)),
            dma((NC, 3)), dma((NC, 3)),
            dma((NC, 6)), dma((NC, 6)),
            dma((NC, 6)), dma((NC, 6)),
            dma((NC, 3)), dma((NC, 3)),
            dma((NC, 3)), dma((NC, 3)),
            dma((NB, 6)), dma((NB, 6)),
            dma((NB, 6)), dma((NB, 6)),
            dma((NB, 3)), dma((NB, 3)),
            dma((NB, 3)), dma((NB, 3)),
        ],
        compiler_params=pltpu.CompilerParams(
            collective_id=0, has_side_effects=True, vmem_limit_bytes=60 * 1024 * 1024
        ),
        cost_estimate=pl.CostEstimate(flops=860_000_000, bytes_accessed=4_500_000, transcendentals=400_000),
        name="latent_decode",
    )(
        query_nope.reshape(ROWS, DN), query_rope.reshape(ROWS, DR), weight_key, weight_value, cache_codes,
        cache_rope.swapaxes(1, 2), cache_scale, lengths, tile_live.T,
    )
    return out.reshape(B, 2, DV)


def solution(mesh):
    in_specs = (
        P("grp", "ctx", None),
        P("grp", "ctx", None),
        P("ctx", None, None),
        P("ctx", None, None),
        P("grp", "ctx", None),
        P("grp", "ctx", None),
        P("grp", "ctx"),
        P("grp"),
        P("grp", "ctx"),
    )
    return jax.shard_map(
        per_device, mesh=mesh, in_specs=in_specs, out_specs=P("grp", "ctx", None), check_vma=False
    )
```

```python
import functools

import jax
import jax.numpy as jnp
from jax import lax
from jax.experimental import pallas as pl
from jax.experimental.pallas import tpu as pltpu
from jax.sharding import PartitionSpec as P

score_factor = 0.0721688
NZ, NY = 16, 4
B, DL, DR, DN, DV = 8, 512, 64, 128, 128
SLOTS, TILE = 384, 128
NB = 1
NC = 4
BC = B // NC
ROWS = 2 * B
PART = DL // NC
QW = DL + 128
HEADS = NY * 2 * NZ
MESH = pl.DeviceIdType.MESH
FAR = (0, 5, -5)
NEAR = (0, 1, -1, 2, -2, 3)
SIZE = (5, 6, 5)
FIRST = (0, 5, 11)
PIECES = ((0, 5), (5, 6), (11, 5))
HANDED = 1
Z_PARTNERS = (5, -5, 3, -3, 2, -2, 1, -1)


def place(f, n):
    return 3 * n + f if n < 5 else 15


Y_OFFS = (2, 1, -1)
f32 = jnp.float32
bf16 = jnp.bfloat16


PLACES = tuple(place(f, n) for f in range(3) for n in range(SIZE[f]))


def kernel(
    qn_hbm, qr_hbm, wk_hbm, wv_hbm, codes_hbm, rope_hbm, scale_hbm, len_hbm, live_hbm, out_ref,
    qn, qr, wk, wv, codes, rope, scales, lens, live,
    qall, zf, obuf, rbuf, sbuf, srbuf, zr, zsend, zrecv, tsend, trecv, mown, msend, mrecv, mtsend, mtrecv,
    zb, bsend, brecv, tb, trb, ysend, yrecv, yt, ytr,
    load_sem, fs, fr, ns, nr, ys, yr, hs, hr, ps, pr, pss, psr, os_, or_, oss, osr, ms, mr, mss, msr, bs, br, bts, btr, es, er, ets, etr,
):
    me = lax.axis_index("ctx")
    z, y = me // NY, lax.rem(me, NY)

    def zid(k):
        return lax.rem(z + k + NZ, NZ)

    def yid(k):
        return lax.rem(y + k + NY, NY)

    def zdev(k):
        return {"ctx": zid(k) * NY + y}

    def ydev(k):
        return {"ctx": z * NY + yid(k)}

    def remote(src, dst, send, recv, device):
        return pltpu.make_async_remote_copy(
            src, dst, send, recv, device_id=device, device_id_type=MESH
        )

    pairs = (
        (qn_hbm, qn), (qr_hbm, qr), (wk_hbm, wk), (codes_hbm, codes), (rope_hbm, rope),
        (scale_hbm, scales), (len_hbm, lens), (live_hbm, live), (wv_hbm, wv),
    )

    def load(i):
        return pltpu.make_async_copy(pairs[i][0], pairs[i][1], load_sem.at[i])

    for i in range(len(pairs)):
        load(i).start()

    barrier = pltpu.get_barrier_semaphore()
    for k in Z_PARTNERS:
        pl.semaphore_signal(barrier, inc=1, device_id=zdev(k), device_id_type=MESH)
    for k in Y_OFFS:
        pl.semaphore_signal(barrier, inc=1, device_id=ydev(k), device_id_type=MESH)

    for i in range(3):
        load(i).wait()
    odd = lax.rem(lax.broadcasted_iota(jnp.int32, (ROWS, DL), 0), 2) == 1
    latent = jnp.where(
        odd,
        jnp.dot(qn[...], wk[1], preferred_element_type=f32),
        jnp.dot(qn[...], wk[0], preferred_element_type=f32),
    )
    qall[y, 0, :, :DL] = latent.astype(bf16)
    qall[y, 0, :, DL:] = jnp.concatenate(
        [qr[...].astype(f32), jnp.zeros((ROWS, 128 - DR), f32)], axis=1
    ).astype(bf16)

    pl.semaphore_wait(barrier, len(Z_PARTNERS) + len(Y_OFFS))

    def far(f):
        return remote(qall.at[y, 0], qall.at[y, FIRST[f]], fs.at[f], fr.at[f], zdev(FAR[f]))

    def near(f, n):
        s = FIRST[f] + n
        return remote(qall.at[y, FIRST[f]], qall.at[y, s], ns.at[s], nr.at[s], zdev(NEAR[n]))

    def ycopy(p, i):
        mine = qall.at[y, pl.ds(*PIECES[p])]
        return remote(mine, mine, ys.at[p, i], yr.at[p, i], ydev((1, -1, 2)[i]))

    def partners(p):
        return range(2 if p == HANDED else 3)

    def hand(i):
        start, size = PIECES[HANDED]
        part = (pl.ds(start + 3, size - 3), pl.ds(start, 3))[i]
        block = qall.at[yid((-1, 1)[i]), part]
        return remote(block, block, hs.at[i], hr.at[i], ydev((1, -1)[i]))

    def near_start(f):
        for n in range(SIZE[f] - 1, 0, -1):
            near(f, n).start()

    def near_wait(f):
        for n in range(1, SIZE[f]):
            near(f, n).wait_recv()

    def y_start(p):
        for i in partners(p):
            ycopy(p, i).start()

    def widen(p):
        if p == HANDED:
            for i in range(2):
                hand(i).wait_recv()
        else:
            for i in range(3):
                ycopy(p, i).wait_recv()
        first, size = PIECES[p]

        def store(v, carry):
            for n in range(size):
                block = qall[v, first + n].astype(f32)
                for j in range(QW // 128):
                    start = pl.multiple_of((v * NZ + PLACES[first + n]) * ROWS, ROWS)
                    zf[j, pl.ds(start, ROWS), :] = block[:, j * 128 : (j + 1) * 128]
            return carry

        lax.fori_loop(0, NY, store, 0)

    far(1).start()
    far(2).start()
    near_start(0)
    near_wait(0)
    y_start(0)
    far(1).wait_recv()
    near_start(1)
    far(2).wait_recv()
    near_start(2)
    near_wait(1)
    y_start(1)
    near_wait(2)
    y_start(2)
    widen(0)
    for i in range(2):
        ycopy(HANDED, i).wait_recv()
        hand(i).start()
    for i in range(3, 8):
        load(i).wait()
    widen(2)
    widen(1)

    def pcopy(c, r, i):
        return remote(
            obuf.at[c, yid(Y_OFFS[i]), r], rbuf.at[c, i, r], ps.at[c, r, i], pr.at[c, r, i], ydev(Y_OFFS[i])
        )

    def scopy(c, i):
        return remote(sbuf.at[c], srbuf.at[c, i], pss.at[c, i], psr.at[c, i], ydev(Y_OFFS[i]))

    lane = lax.broadcasted_iota(jnp.int32, (1, TILE), 1)
    lanes16 = lax.broadcasted_iota(jnp.int32, (NZ, 128), 1)
    eye = lax.broadcasted_iota(jnp.int32, (HEADS, HEADS), 0) == lax.broadcasted_iota(
        jnp.int32, (HEADS, HEADS), 1
    )

    def attend_one(c, r):
        b = c * BC + r
        q = jnp.concatenate(
            [
                jnp.concatenate(
                    [
                        zf[j, pl.ds(v * NZ * ROWS + b * 2 + h, NZ, stride=ROWS), :].astype(bf16)
                        for v in range(NY)
                        for h in range(2)
                    ],
                    axis=0,
                )
                for j in range(QW // 128)
            ],
            axis=1,
        )
        codes_b = codes[b]
        part = lax.dot_general(
            q[:, :DL], codes_b, (((1,), (1,)), ((), ())), preferred_element_type=f32
        )
        turned = jnp.dot(q[:, DL : DL + DR], rope[b], preferred_element_type=f32)
        scale = scales[pl.ds(b, 1), :]
        length = lens[b]
        flags = []
        for t in range(SLOTS // TILE):
            limit = jnp.where(live[t, b] == 1, length - (me * SLOTS + t * TILE), 0)
            flags.append(jnp.where(lane < limit, f32(1.0), f32(0.0)))
        valid = jnp.concatenate(flags, axis=1) > 0.5
        scores = score_factor * (scale * part + turned)
        masked = jnp.where(valid, scores, f32(-1e30))
        top = jnp.max(masked, axis=1, keepdims=True)
        expo = jnp.where(valid, jnp.exp(masked - top), f32(0.0))
        total = jnp.sum(expo, axis=1, keepdims=True)
        probs = (expo * scale).astype(bf16)
        summed = jnp.dot(probs, codes_b, preferred_element_type=f32)
        return top, total, summed

    def attend_y(c, r, carry):
        top, total, summed = attend_one(c, r)
        for v in range(NY):
            obuf[c, v, r] = summed[v * 32 : v * 32 + 32].astype(bf16)
        for i in range(3):
            pcopy(c, r, i).start()
        sbuf[c, r, pl.ds(0, 1), :] = jnp.sum(jnp.where(eye, top, f32(0.0)), axis=0, keepdims=True)
        sbuf[c, r, pl.ds(1, 1), :] = jnp.sum(jnp.where(eye, total, f32(0.0)), axis=0, keepdims=True)
        return carry

    def attend_z(c, r, stats):
        found = attend_one(c, r)
        for v in range(NY):
            for h in range(2):
                mine = slice(v * 32 + h * 16, v * 32 + h * 16 + 16)
                for k in range(NC):
                    zb[pl.ds(v * 256 + k * 2 * BC + r * 2 + h, 16, stride=16), :] = found[2][
                        mine, k * PART : (k + 1) * PART
                    ]
                stats = tuple(
                    jnp.where(lanes16 == r * 2 + h, found[i % 2][mine], old) if i // 2 == v else old
                    for i, old in enumerate(stats)
                )
        return stats

    def pass_on(c):
        for i in range(3):
            scopy(c, i).start()

    rows32 = lax.broadcasted_iota(jnp.int32, (32, 128), 0)
    lanes32 = lax.broadcasted_iota(jnp.int32, (32, 128), 1)
    pick = lanes32 == rows32 + y * 32

    def column(row):
        return jnp.sum(jnp.where(pick, row, f32(0.0)), axis=1, keepdims=True)

    def combine_one(c, r, stats):
        rows = [sbuf[c, r]] + [srbuf[c, i, r] for i in range(3)]
        tops = [column(t[0:1]) for t in rows]
        totals = [column(t[1:2]) for t in rows]
        top = functools.reduce(jnp.maximum, tops)
        factors = [jnp.exp(t - top) for t in tops]
        total = sum(f * t for f, t in zip(factors, totals))
        summed = factors[0] * obuf[c, y, r].astype(f32)
        for i in range(3):
            summed = summed + factors[i + 1] * rbuf[c, i, r].astype(f32)
        first, second = stats
        for h in range(2):
            mine = slice(h * 16, h * 16 + 16)
            for k in range(NC):
                zr[pl.ds(k * 2 * BC + r * 2 + h, 16, stride=16), :] = summed[mine, k * PART : (k + 1) * PART]
            first = jnp.where(lanes16 == r * 2 + h, top[mine], first)
            second = jnp.where(lanes16 == r * 2 + h, total[mine], second)
        return first, second

    def group(n):
        return pl.ds(3 * n, 3) if n < 5 else pl.ds(15, 1)

    def ocopy(c, n):
        part = group(n)
        return remote(zsend.at[c, part], zrecv.at[c, part], os_.at[c, n], or_.at[c, n], zdev(-NEAR[n]))

    def tcopy(c, n):
        part = group(n)
        return remote(tsend.at[c, part], trecv.at[c, part], oss.at[c, n], osr.at[c, n], zdev(-NEAR[n]))

    def mcopy(c, f):
        return remote(msend.at[c, f], mrecv.at[c, f], ms.at[c, f], mr.at[c, f], zdev(-FAR[f]))

    def mtcopy(c, f):
        return remote(mtsend.at[c, f], mtrecv.at[c, f], mss.at[c, f], msr.at[c, f], zdev(-FAR[f]))

    def combine(c, carry):
        for i in range(3):
            scopy(c, i).wait_recv()
            for r in range(BC):
                pcopy(c, r, i).wait_recv()
        blank = jnp.zeros((NZ, 128), f32)
        first, second = lax.fori_loop(0, BC, functools.partial(combine_one, c), (blank, blank))
        for p in range(NZ):
            zsend[c, p] = zr[pl.ds(p * 16, 16), :].astype(bf16)
            tsend[c, p, 0:1, :] = first[p : p + 1]
            tsend[c, p, 1:2, :] = second[p : p + 1]
        for n in range(5, 0, -1):
            tcopy(c, n).start()
            ocopy(c, n).start()
        return carry

    spot = lanes16 == lax.rem(lax.broadcasted_iota(jnp.int32, (ROWS, 128), 0), 2 * BC)

    def spread_out(row):
        return jnp.sum(jnp.where(spot, row, f32(0.0)), axis=1, keepdims=True)

    def merge_rows(own, others, blocks):
        tops = [own[0]] + [t[0] for t in others]
        totals = [own[1]] + [t[1] for t in others]
        top = functools.reduce(jnp.maximum, tops)
        weights = [jnp.exp(t - top) for t in tops]
        whole = sum(w * t for w, t in zip(weights, totals))
        return top, whole, sum(spread_out(w) * block.astype(f32) for w, block in zip(weights, blocks))

    def merge(stats, blocks):
        rows = [(t[0:1], t[1:2]) for t in stats]
        return merge_rows(rows[0], rows[1:], blocks)

    def forward(c, f, top, whole, summed):
        mtsend[c, f, 0:1, :] = top
        mtsend[c, f, 1:2, :] = whole
        if f == 0:
            mown[c] = summed
        else:
            msend[c, f] = summed.astype(bf16)
            mtcopy(c, f).start()
            mcopy(c, f).start()

    def middle(c, carry):
        for n in range(1, 6):
            tcopy(c, n).wait_recv()
            ocopy(c, n).wait_recv()
        for f in (1, 2, 0):
            places = [place(f, n) for n in range(1, SIZE[f])]
            merged = merge(
                [tsend[c, f]] + [trecv[c, p] for p in places],
                [zsend[c, f]] + [zrecv[c, p] for p in places],
            )
            forward(c, f, *merged)
        return carry

    def bcopy(c, n):
        part = group(n)
        return remote(bsend.at[c, part], brecv.at[c, part], bs.at[c, n], br.at[c, n], zdev(-NEAR[n]))

    def btcopy(c, n):
        part = pl.ds(24 * n, 24) if n < 5 else pl.ds(120, 8)
        return remote(tb.at[c, part], trb.at[c, part], bts.at[c, n], btr.at[c, n], zdev(-NEAR[n]))

    def ecopy(c, i):
        return remote(
            ysend.at[c, yid(Y_OFFS[i])], yrecv.at[c, i], es.at[c, i], er.at[c, i], ydev(Y_OFFS[i])
        )

    def etcopy(c, i):
        return remote(yt.at[c, yid(Y_OFFS[i])], ytr.at[c, i], ets.at[c, i], etr.at[c, i], ydev(Y_OFFS[i]))

    def z_first(c, carry):
        stats = (jnp.zeros((NZ, 128), f32),) * (2 * NY)
        stats = lax.fori_loop(0, BC, functools.partial(attend_z, c), stats)
        for i in range(2 * NY):
            tb[c, pl.ds(i, NZ, stride=8), :] = stats[i]

        def pack(v, carry):
            for p in range(NZ):
                bsend[c, p, v] = zb[pl.ds(pl.multiple_of(v * 256 + p * 16, 16), 16), :].astype(bf16)
            return carry

        lax.fori_loop(0, NY, pack, 0)
        for n in range(5, 0, -1):
            btcopy(c, n).start()
            bcopy(c, n).start()
        return carry

    def z_middle(c, carry):
        for n in range(1, 6):
            btcopy(c, n).wait_recv()
            bcopy(c, n).wait_recv()

        def one(v, carry):
            for f in range(3):
                places = [place(f, n) for n in range(1, SIZE[f])]
                top, whole, summed = merge_rows(
                    [tb[c, pl.ds(f * 8 + v * 2 + m, 1), :] for m in range(2)],
                    [[trb[c, pl.ds(p * 8 + v * 2 + m, 1), :] for m in range(2)] for p in places],
                    [bsend[c, f, v]] + [brecv[c, p, v] for p in places],
                )
                ysend[c, v, f] = summed.astype(bf16)
                yt[c, v, f * 2 : f * 2 + 1, :] = top
                yt[c, v, f * 2 + 1 : f * 2 + 2, :] = whole
            return carry

        lax.fori_loop(0, NY, one, 0)
        for i in range(3):
            etcopy(c, i).start()
            ecopy(c, i).start()
        return carry

    def z_last(c, carry):
        for i in range(3):
            etcopy(c, i).wait_recv()
            ecopy(c, i).wait_recv()
        for f in (1, 2, 0):
            merged = merge_rows(
                [yt[c, y, f * 2 + m : f * 2 + m + 1, :] for m in range(2)],
                [[ytr[c, i, f * 2 + m : f * 2 + m + 1, :] for m in range(2)] for i in range(3)],
                [ysend[c, y, f]] + [yrecv[c, i, f] for i in range(3)],
            )
            forward(c, f, *merged)
        return carry

    def y_first(c, carry):
        lax.fori_loop(0, BC, functools.partial(attend_y, c), 0)
        pass_on(c)
        return carry

    lax.fori_loop(0, NB, z_first, 0)
    lax.fori_loop(NB, NC, y_first, 0)
    lax.fori_loop(0, NB, z_middle, 0)
    lax.fori_loop(NB, NC, combine, 0)
    lax.fori_loop(0, NB, z_last, 0)
    lax.fori_loop(NB, NC, middle, 0)

    load(8).wait()
    odd16 = lax.rem(lax.broadcasted_iota(jnp.int32, (ROWS, DV), 0), 2) == 1
    finished = []
    for c in range(NC):
        for f in (1, 2):
            mtcopy(c, f).wait_recv()
            mcopy(c, f).wait_recv()
        _, whole, summed = merge(
            [mtsend[c, 0], mtrecv[c, 1], mtrecv[c, 2]], [mown[c], mrecv[c, 1], mrecv[c, 2]]
        )
        summed = summed / spread_out(whole)
        finished.append(
            jnp.concatenate([summed[k * 2 * BC : (k + 1) * 2 * BC] for k in range(NC)], axis=1)
        )
    latent_out = jnp.concatenate(finished, axis=0).astype(bf16)
    out_ref[...] = jnp.where(
        odd16,
        jnp.dot(latent_out, wv[1], preferred_element_type=f32),
        jnp.dot(latent_out, wv[0], preferred_element_type=f32),
    ).astype(bf16)

    for f in range(3):
        if f:
            far(f).wait_send()
        for n in range(1, SIZE[f]):
            near(f, n).wait_send()
    for p in range(len(PIECES)):
        for i in partners(p):
            ycopy(p, i).wait_send()
    for i in range(2):
        hand(i).wait_send()

    def drain_y(c, carry):
        for i in range(3):
            for r in range(BC):
                pcopy(c, r, i).wait_send()
            scopy(c, i).wait_send()
        for n in range(1, 6):
            tcopy(c, n).wait_send()
            ocopy(c, n).wait_send()
        return carry

    def drain_z(c, carry):
        for n in range(1, 6):
            btcopy(c, n).wait_send()
            bcopy(c, n).wait_send()
        for i in range(3):
            etcopy(c, i).wait_send()
            ecopy(c, i).wait_send()
        return carry

    def drain(c, carry):
        for f in (1, 2):
            mtcopy(c, f).wait_send()
            mcopy(c, f).wait_send()
        return carry

    lax.fori_loop(0, NB, drain_z, 0)
    lax.fori_loop(NB, NC, drain_y, 0)
    lax.fori_loop(0, NC, drain, 0)


def per_device(
    query_nope, query_rope, weight_key, weight_value, cache_codes, cache_rope, cache_scale, lengths, tile_live
):
    hbm = pl.BlockSpec(memory_space=pl.ANY)
    dma = pltpu.SemaphoreType.DMA
    vmem = pltpu.VMEM
    out = pl.pallas_call(
        kernel,
        out_shape=jax.ShapeDtypeStruct((ROWS, DV), bf16),
        in_specs=[hbm] * 9,
        out_specs=pl.BlockSpec(memory_space=pltpu.VMEM),
        scratch_shapes=[
            vmem((ROWS, DN), bf16),
            vmem((ROWS, DR), bf16),
            vmem((2, DN, DL), bf16),
            vmem((2, DL, DV), bf16),
            vmem((B, SLOTS, DL), bf16),
            vmem((B, DR, SLOTS), bf16),
            vmem((B, SLOTS), f32),
            pltpu.SMEM((B,), jnp.int32),
            pltpu.SMEM((SLOTS // TILE, B), jnp.int32),
            vmem((NY, NZ, ROWS, QW), bf16),
            vmem((QW // 128, NY * NZ * ROWS, 128), f32),
            vmem((NC, NY, BC, 32, DL), bf16),
            vmem((NC, 3, BC, 32, DL), bf16),
            vmem((NC, BC, 2, 128), f32),
            vmem((NC, 3, BC, 2, 128), f32),
            vmem((NZ * 16, PART), f32),
            vmem((NC, NZ, 16, PART), bf16),
            vmem((NC, NZ, 16, PART), bf16),
            vmem((NC, NZ, 2, 128), f32),
            vmem((NC, NZ, 2, 128), f32),
            vmem((NC, 16, PART), f32),
            vmem((NC, 3, 16, PART), bf16),
            vmem((NC, 3, 16, PART), bf16),
            vmem((NC, 3, 2, 128), f32),
            vmem((NC, 3, 2, 128), f32),
            vmem((NY * NZ * 16, PART), f32),
            vmem((NB, NZ, NY, 16, PART), bf16),
            vmem((NB, NZ, NY, 16, PART), bf16),
            vmem((NB, NZ * 8, 128), f32),
            vmem((NB, NZ * 8, 128), f32),
            vmem((NB, NY, 3, 16, PART), bf16),
            vmem((NB, 3, 3, 16, PART), bf16),
            vmem((NB, NY, 8, 128), f32),
            vmem((NB, 3, 8, 128), f32),
            dma((9,)),
            dma((3,)), dma((3,)),
            dma((NZ,)), dma((NZ,)),
            dma((len(PIECES), 3)), dma((len(PIECES), 3)),
            dma((2,)), dma((2,)),
            dma((NC, BC, 3)), dma((NC, BC, 3)),
            dma((NC, 3)), dma((NC, 3)),
            dma((NC, 6)), dma((NC, 6)),
            dma((NC, 6)), dma((NC, 6)),
            dma((NC, 3)), dma((NC, 3)),
            dma((NC, 3)), dma((NC, 3)),
            dma((NB, 6)), dma((NB, 6)),
            dma((NB, 6)), dma((NB, 6)),
            dma((NB, 3)), dma((NB, 3)),
            dma((NB, 3)), dma((NB, 3)),
        ],
        compiler_params=pltpu.CompilerParams(
            collective_id=0, has_side_effects=True, vmem_limit_bytes=60 * 1024 * 1024
        ),
        cost_estimate=pl.CostEstimate(flops=860_000_000, bytes_accessed=4_500_000, transcendentals=400_000),
        name="latent_decode",
    )(
        query_nope.reshape(ROWS, DN), query_rope.reshape(ROWS, DR), weight_key, weight_value, cache_codes,
        cache_rope.swapaxes(1, 2), cache_scale, lengths, tile_live.T,
    )
    return out.reshape(B, 2, DV)


def solution(mesh):
    in_specs = (
        P("grp", "ctx", None),
        P("grp", "ctx", None),
        P("ctx", None, None),
        P("ctx", None, None),
        P("grp", "ctx", None),
        P("grp", "ctx", None),
        P("grp", "ctx"),
        P("grp"),
        P("grp", "ctx"),
    )
    return jax.shard_map(
        per_device, mesh=mesh, in_specs=in_specs, out_specs=P("grp", "ctx", None), check_vma=False
    )
```

```python
import functools

import jax
import jax.numpy as jnp
from jax import lax
from jax.experimental import pallas as pl
from jax.experimental.pallas import tpu as pltpu
from jax.sharding import PartitionSpec as P

score_factor = 0.0721688
NZ, NY = 16, 4
B, DL, DR, DN, DV = 8, 512, 64, 128, 128
SLOTS, TILE = 384, 128
NB = 1
NC = 4
BC = B // NC
ROWS = 2 * B
PART = DL // NC
QW = DL + 128
HEADS = NY * 2 * NZ
MESH = pl.DeviceIdType.MESH
FAR = (0, 5, -5)
NEAR = (0, 1, -1, 2, -2, 3)
SIZE = (5, 6, 5)
FIRST = (0, 5, 11)
PIECES = ((0, 5), (5, 6), (11, 5))
HANDED = 1
Z_PARTNERS = (5, -5, 3, -3, 2, -2, 1, -1)


def place(f, n):
    return 3 * n + f if n < 5 else 15


Y_OFFS = (2, 1, -1)
f32 = jnp.float32
bf16 = jnp.bfloat16


PLACES = tuple(place(f, n) for f in range(3) for n in range(SIZE[f]))


def kernel(
    qn_hbm, qr_hbm, wk_hbm, wv_hbm, codes_hbm, rope_hbm, scale_hbm, len_hbm, live_hbm, out_ref,
    qn, qr, wk, wv, codes, rope, scales, lens, live,
    qall, zf, obuf, rbuf, sbuf, srbuf, zr, zsend, zrecv, tsend, trecv, mown, msend, mrecv, mtsend, mtrecv,
    zb, bsend, brecv, tb, trb, ysend, yrecv, yt, ytr,
    load_sem, fs, fr, ns, nr, ys, yr, hs, hr, ps, pr, pss, psr, os_, or_, oss, osr, ms, mr, mss, msr, bs, br, bts, btr, es, er, ets, etr,
):
    me = lax.axis_index("ctx")
    z, y = me // NY, lax.rem(me, NY)

    def zid(k):
        return lax.rem(z + k + NZ, NZ)

    def yid(k):
        return lax.rem(y + k + NY, NY)

    def zdev(k):
        return {"ctx": zid(k) * NY + y}

    def ydev(k):
        return {"ctx": z * NY + yid(k)}

    def remote(src, dst, send, recv, device):
        return pltpu.make_async_remote_copy(
            src, dst, send, recv, device_id=device, device_id_type=MESH
        )

    pairs = (
        (qn_hbm, qn), (qr_hbm, qr), (wk_hbm, wk), (codes_hbm, codes), (rope_hbm, rope),
        (scale_hbm, scales), (len_hbm, lens), (live_hbm, live), (wv_hbm, wv),
    )

    def load(i):
        return pltpu.make_async_copy(pairs[i][0], pairs[i][1], load_sem.at[i])

    for i in range(3):
        load(i).start()

    barrier = pltpu.get_barrier_semaphore()
    for k in Z_PARTNERS:
        pl.semaphore_signal(barrier, inc=1, device_id=zdev(k), device_id_type=MESH)
    for k in Y_OFFS:
        pl.semaphore_signal(barrier, inc=1, device_id=ydev(k), device_id_type=MESH)

    for i in range(3, len(pairs)):
        load(i).start()

    for i in range(3):
        load(i).wait()
    odd = lax.rem(lax.broadcasted_iota(jnp.int32, (ROWS, DL), 0), 2) == 1
    latent = jnp.where(
        odd,
        jnp.dot(qn[...], wk[1], preferred_element_type=f32),
        jnp.dot(qn[...], wk[0], preferred_element_type=f32),
    )
    qall[y, 0, :, :DL] = latent.astype(bf16)
    qall[y, 0, :, DL:] = jnp.concatenate(
        [qr[...].astype(f32), jnp.zeros((ROWS, 128 - DR), f32)], axis=1
    ).astype(bf16)

    pl.semaphore_wait(barrier, len(Z_PARTNERS) + len(Y_OFFS))

    def far(f):
        return remote(qall.at[y, 0], qall.at[y, FIRST[f]], fs.at[f], fr.at[f], zdev(FAR[f]))

    def near(f, n):
        s = FIRST[f] + n
        return remote(qall.at[y, FIRST[f]], qall.at[y, s], ns.at[s], nr.at[s], zdev(NEAR[n]))

    def ycopy(p, i):
        mine = qall.at[y, pl.ds(*PIECES[p])]
        return remote(mine, mine, ys.at[p, i], yr.at[p, i], ydev((1, -1, 2)[i]))

    def partners(p):
        return range(2 if p == HANDED else 3)

    def hand(i):
        start, size = PIECES[HANDED]
        part = (pl.ds(start + 3, size - 3), pl.ds(start, 3))[i]
        block = qall.at[yid((-1, 1)[i]), part]
        return remote(block, block, hs.at[i], hr.at[i], ydev((1, -1)[i]))

    def near_start(f):
        for n in range(SIZE[f] - 1, 0, -1):
            near(f, n).start()

    def near_wait(f):
        for n in range(1, SIZE[f]):
            near(f, n).wait_recv()

    def y_start(p):
        for i in partners(p):
            ycopy(p, i).start()

    def widen(p):
        if p == HANDED:
            for i in range(2):
                hand(i).wait_recv()
        else:
            for i in range(3):
                ycopy(p, i).wait_recv()
        first, size = PIECES[p]

        def store(v, carry):
            for n in range(size):
                block = qall[v, first + n].astype(f32)
                for j in range(QW // 128):
                    start = pl.multiple_of((v * NZ + PLACES[first + n]) * ROWS, ROWS)
                    zf[j, pl.ds(start, ROWS), :] = block[:, j * 128 : (j + 1) * 128]
            return carry

        lax.fori_loop(0, NY, store, 0)

    far(1).start()
    far(2).start()
    near_start(0)
    near_wait(0)
    y_start(0)
    far(1).wait_recv()
    near_start(1)
    far(2).wait_recv()
    near_start(2)
    near_wait(1)
    y_start(1)
    near_wait(2)
    y_start(2)
    widen(0)
    for i in range(2):
        ycopy(HANDED, i).wait_recv()
        hand(i).start()
    for i in range(3, 8):
        load(i).wait()
    widen(2)
    widen(1)

    def pcopy(c, r, i):
        return remote(
            obuf.at[c, yid(Y_OFFS[i]), r], rbuf.at[c, i, r], ps.at[c, r, i], pr.at[c, r, i], ydev(Y_OFFS[i])
        )

    def scopy(c, i):
        return remote(sbuf.at[c], srbuf.at[c, i], pss.at[c, i], psr.at[c, i], ydev(Y_OFFS[i]))

    lane = lax.broadcasted_iota(jnp.int32, (1, TILE), 1)
    lanes16 = lax.broadcasted_iota(jnp.int32, (NZ, 128), 1)
    eye = lax.broadcasted_iota(jnp.int32, (HEADS, HEADS), 0) == lax.broadcasted_iota(
        jnp.int32, (HEADS, HEADS), 1
    )

    def attend_one(c, r):
        b = c * BC + r
        q = jnp.concatenate(
            [
                jnp.concatenate(
                    [
                        zf[j, pl.ds(v * NZ * ROWS + b * 2 + h, NZ, stride=ROWS), :].astype(bf16)
                        for v in range(NY)
                        for h in range(2)
                    ],
                    axis=0,
                )
                for j in range(QW // 128)
            ],
            axis=1,
        )
        codes_b = codes[b]
        part = lax.dot_general(
            q[:, :DL], codes_b, (((1,), (1,)), ((), ())), preferred_element_type=f32
        )
        turned = jnp.dot(q[:, DL : DL + DR], rope[b], preferred_element_type=f32)
        scale = scales[pl.ds(b, 1), :]
        length = lens[b]
        flags = []
        for t in range(SLOTS // TILE):
            limit = jnp.where(live[t, b] == 1, length - (me * SLOTS + t * TILE), 0)
            flags.append(jnp.where(lane < limit, f32(1.0), f32(0.0)))
        valid = jnp.concatenate(flags, axis=1) > 0.5
        scores = score_factor * (scale * part + turned)
        masked = jnp.where(valid, scores, f32(-1e30))
        top = jnp.max(masked, axis=1, keepdims=True)
        expo = jnp.where(valid, jnp.exp(masked - top), f32(0.0))
        total = jnp.sum(expo, axis=1, keepdims=True)
        probs = (expo * scale).astype(bf16)
        summed = jnp.dot(probs, codes_b, preferred_element_type=f32)
        return top, total, summed

    def attend_y(c, r, carry):
        top, total, summed = attend_one(c, r)
        for v in range(NY):
            obuf[c, v, r] = summed[v * 32 : v * 32 + 32].astype(bf16)
        for i in range(3):
            pcopy(c, r, i).start()
        sbuf[c, r, pl.ds(0, 1), :] = jnp.sum(jnp.where(eye, top, f32(0.0)), axis=0, keepdims=True)
        sbuf[c, r, pl.ds(1, 1), :] = jnp.sum(jnp.where(eye, total, f32(0.0)), axis=0, keepdims=True)
        return carry

    def attend_z(c, r, stats):
        found = attend_one(c, r)
        for v in range(NY):
            for h in range(2):
                mine = slice(v * 32 + h * 16, v * 32 + h * 16 + 16)
                for k in range(NC):
                    zb[pl.ds(v * 256 + k * 2 * BC + r * 2 + h, 16, stride=16), :] = found[2][
                        mine, k * PART : (k + 1) * PART
                    ]
                stats = tuple(
                    jnp.where(lanes16 == r * 2 + h, found[i % 2][mine], old) if i // 2 == v else old
                    for i, old in enumerate(stats)
                )
        return stats

    def pass_on(c):
        for i in range(3):
            scopy(c, i).start()

    rows32 = lax.broadcasted_iota(jnp.int32, (32, 128), 0)
    lanes32 = lax.broadcasted_iota(jnp.int32, (32, 128), 1)
    pick = lanes32 == rows32 + y * 32

    def column(row):
        return jnp.sum(jnp.where(pick, row, f32(0.0)), axis=1, keepdims=True)

    def combine_one(c, r, stats):
        rows = [sbuf[c, r]] + [srbuf[c, i, r] for i in range(3)]
        tops = [column(t[0:1]) for t in rows]
        totals = [column(t[1:2]) for t in rows]
        top = functools.reduce(jnp.maximum, tops)
        factors = [jnp.exp(t - top) for t in tops]
        total = sum(f * t for f, t in zip(factors, totals))
        summed = factors[0] * obuf[c, y, r].astype(f32)
        for i in range(3):
            summed = summed + factors[i + 1] * rbuf[c, i, r].astype(f32)
        first, second = stats
        for h in range(2):
            mine = slice(h * 16, h * 16 + 16)
            for k in range(NC):
                zr[pl.ds(k * 2 * BC + r * 2 + h, 16, stride=16), :] = summed[mine, k * PART : (k + 1) * PART]
            first = jnp.where(lanes16 == r * 2 + h, top[mine], first)
            second = jnp.where(lanes16 == r * 2 + h, total[mine], second)
        return first, second

    def group(n):
        return pl.ds(3 * n, 3) if n < 5 else pl.ds(15, 1)

    def ocopy(c, n):
        part = group(n)
        return remote(zsend.at[c, part], zrecv.at[c, part], os_.at[c, n], or_.at[c, n], zdev(-NEAR[n]))

    def tcopy(c, n):
        part = group(n)
        return remote(tsend.at[c, part], trecv.at[c, part], oss.at[c, n], osr.at[c, n], zdev(-NEAR[n]))

    def mcopy(c, f):
        return remote(msend.at[c, f], mrecv.at[c, f], ms.at[c, f], mr.at[c, f], zdev(-FAR[f]))

    def mtcopy(c, f):
        return remote(mtsend.at[c, f], mtrecv.at[c, f], mss.at[c, f], msr.at[c, f], zdev(-FAR[f]))

    def combine(c, carry):
        for i in range(3):
            scopy(c, i).wait_recv()
            for r in range(BC):
                pcopy(c, r, i).wait_recv()
        blank = jnp.zeros((NZ, 128), f32)
        first, second = lax.fori_loop(0, BC, functools.partial(combine_one, c), (blank, blank))
        for p in range(NZ):
            zsend[c, p] = zr[pl.ds(p * 16, 16), :].astype(bf16)
            tsend[c, p, 0:1, :] = first[p : p + 1]
            tsend[c, p, 1:2, :] = second[p : p + 1]
        for n in range(5, 0, -1):
            tcopy(c, n).start()
            ocopy(c, n).start()
        return carry

    spot = lanes16 == lax.rem(lax.broadcasted_iota(jnp.int32, (ROWS, 128), 0), 2 * BC)

    def spread_out(row):
        return jnp.sum(jnp.where(spot, row, f32(0.0)), axis=1, keepdims=True)

    def merge_rows(own, others, blocks):
        tops = [own[0]] + [t[0] for t in others]
        totals = [own[1]] + [t[1] for t in others]
        top = functools.reduce(jnp.maximum, tops)
        weights = [jnp.exp(t - top) for t in tops]
        whole = sum(w * t for w, t in zip(weights, totals))
        return top, whole, sum(spread_out(w) * block.astype(f32) for w, block in zip(weights, blocks))

    def merge(stats, blocks):
        rows = [(t[0:1], t[1:2]) for t in stats]
        return merge_rows(rows[0], rows[1:], blocks)

    def forward(c, f, top, whole, summed):
        mtsend[c, f, 0:1, :] = top
        mtsend[c, f, 1:2, :] = whole
        if f == 0:
            mown[c] = summed
        else:
            msend[c, f] = summed.astype(bf16)
            mtcopy(c, f).start()
            mcopy(c, f).start()

    def middle(c, carry):
        for n in range(1, 6):
            tcopy(c, n).wait_recv()
            ocopy(c, n).wait_recv()
        for f in (1, 2, 0):
            places = [place(f, n) for n in range(1, SIZE[f])]
            merged = merge(
                [tsend[c, f]] + [trecv[c, p] for p in places],
                [zsend[c, f]] + [zrecv[c, p] for p in places],
            )
            forward(c, f, *merged)
        return carry

    def bcopy(c, n):
        part = group(n)
        return remote(bsend.at[c, part], brecv.at[c, part], bs.at[c, n], br.at[c, n], zdev(-NEAR[n]))

    def btcopy(c, n):
        part = pl.ds(24 * n, 24) if n < 5 else pl.ds(120, 8)
        return remote(tb.at[c, part], trb.at[c, part], bts.at[c, n], btr.at[c, n], zdev(-NEAR[n]))

    def ecopy(c, i):
        return remote(
            ysend.at[c, yid(Y_OFFS[i])], yrecv.at[c, i], es.at[c, i], er.at[c, i], ydev(Y_OFFS[i])
        )

    def etcopy(c, i):
        return remote(yt.at[c, yid(Y_OFFS[i])], ytr.at[c, i], ets.at[c, i], etr.at[c, i], ydev(Y_OFFS[i]))

    def z_first(c, carry):
        stats = (jnp.zeros((NZ, 128), f32),) * (2 * NY)
        stats = lax.fori_loop(0, BC, functools.partial(attend_z, c), stats)
        for i in range(2 * NY):
            tb[c, pl.ds(i, NZ, stride=8), :] = stats[i]

        def pack(v, carry):
            for p in range(NZ):
                bsend[c, p, v] = zb[pl.ds(pl.multiple_of(v * 256 + p * 16, 16), 16), :].astype(bf16)
            return carry

        lax.fori_loop(0, NY, pack, 0)
        for n in range(5, 0, -1):
            btcopy(c, n).start()
            bcopy(c, n).start()
        return carry

    def z_middle(c, carry):
        for n in range(1, 6):
            btcopy(c, n).wait_recv()
            bcopy(c, n).wait_recv()

        def one(v, carry):
            for f in range(3):
                places = [place(f, n) for n in range(1, SIZE[f])]
                top, whole, summed = merge_rows(
                    [tb[c, pl.ds(f * 8 + v * 2 + m, 1), :] for m in range(2)],
                    [[trb[c, pl.ds(p * 8 + v * 2 + m, 1), :] for m in range(2)] for p in places],
                    [bsend[c, f, v]] + [brecv[c, p, v] for p in places],
                )
                ysend[c, v, f] = summed.astype(bf16)
                yt[c, v, f * 2 : f * 2 + 1, :] = top
                yt[c, v, f * 2 + 1 : f * 2 + 2, :] = whole
            return carry

        lax.fori_loop(0, NY, one, 0)
        for i in range(3):
            etcopy(c, i).start()
            ecopy(c, i).start()
        return carry

    def z_last(c, carry):
        for i in range(3):
            etcopy(c, i).wait_recv()
            ecopy(c, i).wait_recv()
        for f in (1, 2, 0):
            merged = merge_rows(
                [yt[c, y, f * 2 + m : f * 2 + m + 1, :] for m in range(2)],
                [[ytr[c, i, f * 2 + m : f * 2 + m + 1, :] for m in range(2)] for i in range(3)],
                [ysend[c, y, f]] + [yrecv[c, i, f] for i in range(3)],
            )
            forward(c, f, *merged)
        return carry

    def y_first(c, carry):
        lax.fori_loop(0, BC, functools.partial(attend_y, c), 0)
        pass_on(c)
        return carry

    lax.fori_loop(0, NB, z_first, 0)
    lax.fori_loop(NB, NC, y_first, 0)
    lax.fori_loop(0, NB, z_middle, 0)
    lax.fori_loop(NB, NC, combine, 0)
    lax.fori_loop(0, NB, z_last, 0)
    lax.fori_loop(NB, NC, middle, 0)

    load(8).wait()
    odd16 = lax.rem(lax.broadcasted_iota(jnp.int32, (ROWS, DV), 0), 2) == 1
    finished = []
    for c in range(NC):
        for f in (1, 2):
            mtcopy(c, f).wait_recv()
            mcopy(c, f).wait_recv()
        _, whole, summed = merge(
            [mtsend[c, 0], mtrecv[c, 1], mtrecv[c, 2]], [mown[c], mrecv[c, 1], mrecv[c, 2]]
        )
        summed = summed / spread_out(whole)
        finished.append(
            jnp.concatenate([summed[k * 2 * BC : (k + 1) * 2 * BC] for k in range(NC)], axis=1)
        )
    latent_out = jnp.concatenate(finished, axis=0).astype(bf16)
    out_ref[...] = jnp.where(
        odd16,
        jnp.dot(latent_out, wv[1], preferred_element_type=f32),
        jnp.dot(latent_out, wv[0], preferred_element_type=f32),
    ).astype(bf16)

    for f in range(3):
        if f:
            far(f).wait_send()
        for n in range(1, SIZE[f]):
            near(f, n).wait_send()
    for p in range(len(PIECES)):
        for i in partners(p):
            ycopy(p, i).wait_send()
    for i in range(2):
        hand(i).wait_send()

    def drain_y(c, carry):
        for i in range(3):
            for r in range(BC):
                pcopy(c, r, i).wait_send()
            scopy(c, i).wait_send()
        for n in range(1, 6):
            tcopy(c, n).wait_send()
            ocopy(c, n).wait_send()
        return carry

    def drain_z(c, carry):
        for n in range(1, 6):
            btcopy(c, n).wait_send()
            bcopy(c, n).wait_send()
        for i in range(3):
            etcopy(c, i).wait_send()
            ecopy(c, i).wait_send()
        return carry

    def drain(c, carry):
        for f in (1, 2):
            mtcopy(c, f).wait_send()
            mcopy(c, f).wait_send()
        return carry

    lax.fori_loop(0, NB, drain_z, 0)
    lax.fori_loop(NB, NC, drain_y, 0)
    lax.fori_loop(0, NC, drain, 0)


def per_device(
    query_nope, query_rope, weight_key, weight_value, cache_codes, cache_rope, cache_scale, lengths, tile_live
):
    hbm = pl.BlockSpec(memory_space=pl.ANY)
    dma = pltpu.SemaphoreType.DMA
    vmem = pltpu.VMEM
    out = pl.pallas_call(
        kernel,
        out_shape=jax.ShapeDtypeStruct((ROWS, DV), bf16),
        in_specs=[hbm] * 9,
        out_specs=pl.BlockSpec(memory_space=pltpu.VMEM),
        scratch_shapes=[
            vmem((ROWS, DN), bf16),
            vmem((ROWS, DR), bf16),
            vmem((2, DN, DL), bf16),
            vmem((2, DL, DV), bf16),
            vmem((B, SLOTS, DL), bf16),
            vmem((B, DR, SLOTS), bf16),
            vmem((B, SLOTS), f32),
            pltpu.SMEM((B,), jnp.int32),
            pltpu.SMEM((SLOTS // TILE, B), jnp.int32),
            vmem((NY, NZ, ROWS, QW), bf16),
            vmem((QW // 128, NY * NZ * ROWS, 128), f32),
            vmem((NC, NY, BC, 32, DL), bf16),
            vmem((NC, 3, BC, 32, DL), bf16),
            vmem((NC, BC, 2, 128), f32),
            vmem((NC, 3, BC, 2, 128), f32),
            vmem((NZ * 16, PART), f32),
            vmem((NC, NZ, 16, PART), bf16),
            vmem((NC, NZ, 16, PART), bf16),
            vmem((NC, NZ, 2, 128), f32),
            vmem((NC, NZ, 2, 128), f32),
            vmem((NC, 16, PART), f32),
            vmem((NC, 3, 16, PART), bf16),
            vmem((NC, 3, 16, PART), bf16),
            vmem((NC, 3, 2, 128), f32),
            vmem((NC, 3, 2, 128), f32),
            vmem((NY * NZ * 16, PART), f32),
            vmem((NB, NZ, NY, 16, PART), bf16),
            vmem((NB, NZ, NY, 16, PART), bf16),
            vmem((NB, NZ * 8, 128), f32),
            vmem((NB, NZ * 8, 128), f32),
            vmem((NB, NY, 3, 16, PART), bf16),
            vmem((NB, 3, 3, 16, PART), bf16),
            vmem((NB, NY, 8, 128), f32),
            vmem((NB, 3, 8, 128), f32),
            dma((9,)),
            dma((3,)), dma((3,)),
            dma((NZ,)), dma((NZ,)),
            dma((len(PIECES), 3)), dma((len(PIECES), 3)),
            dma((2,)), dma((2,)),
            dma((NC, BC, 3)), dma((NC, BC, 3)),
            dma((NC, 3)), dma((NC, 3)),
            dma((NC, 6)), dma((NC, 6)),
            dma((NC, 6)), dma((NC, 6)),
            dma((NC, 3)), dma((NC, 3)),
            dma((NC, 3)), dma((NC, 3)),
            dma((NB, 6)), dma((NB, 6)),
            dma((NB, 6)), dma((NB, 6)),
            dma((NB, 3)), dma((NB, 3)),
            dma((NB, 3)), dma((NB, 3)),
        ],
        compiler_params=pltpu.CompilerParams(
            collective_id=0, has_side_effects=True, vmem_limit_bytes=60 * 1024 * 1024
        ),
        cost_estimate=pl.CostEstimate(flops=860_000_000, bytes_accessed=4_500_000, transcendentals=400_000),
        name="latent_decode",
    )(
        query_nope.reshape(ROWS, DN), query_rope.reshape(ROWS, DR), weight_key, weight_value, cache_codes,
        cache_rope.swapaxes(1, 2), cache_scale, lengths, tile_live.T,
    )
    return out.reshape(B, 2, DV)


def solution(mesh):
    in_specs = (
        P("grp", "ctx", None),
        P("grp", "ctx", None),
        P("ctx", None, None),
        P("ctx", None, None),
        P("grp", "ctx", None),
        P("grp", "ctx", None),
        P("grp", "ctx"),
        P("grp"),
        P("grp", "ctx"),
    )
    return jax.shard_map(
        per_device, mesh=mesh, in_specs=in_specs, out_specs=P("grp", "ctx", None), check_vma=False
    )
```
